32 devices in a mesh: band: 4 (over y, x), lon: 8 (over z, core).
Axes of the slice: x: 2, y: 2, z: 4, core: 2. Of those that a mesh axis runs over, the one named last changes fastest.
Arguments:
- latent: bfloat16 [128, 1024, 256], P('band', 'lon'), may hold values from -6 to 6
- row_index: int32 [4, 8, 16], P('band', 'lon'), may hold values from 0 to 31
- interp_weights: bfloat16 [512, 128, 128], P(('band', 'lon')), may hold values from -0.5 to 0.5
- observation_slot_index: int32 [512, 128], P(('band', 'lon')), may hold values from 0 to 6
- counts: int32 [512], P(('band', 'lon')), may hold values from 32 to 128
- targets: bfloat16 [512, 128, 128], P(('band', 'lon')), may hold values from -6 to 6
- gain: float32 [256], replicated, may hold values from 0.5 to 1.5
- w_in: bfloat16 [256, 512], replicated, may hold values from -0.375 to 0.375
- w_out: bfloat16 [512, 256], replicated, may hold values from -0.25 to 0.25
- head: bfloat16 [256, 128], replicated, may hold values from -0.375 to 0.375
Outputs:
- grad_latent: float32 [128, 1024, 256], P('band', 'lon')
- grad_w_in: float32 [256, 512], replicated
- grad_w_out: float32 [512, 256], replicated
- grad_gain: float32 [256], replicated
- grad_head: float32 [256, 128], replicated
The draws below stay inside these ranges and needn't reach their ends.
All inputs are finite; a program needn't handle non-finite values.
Results may differ from the reference program's by a relative error of at most 0.007.
Values may be sent and summed in bfloat16 or wider, within the bound.
A program may use at most 128 MiB of HBM per device.

```python
import math
import jax
import jax.numpy as jnp
from jax import lax

C = 256
HID = 512
NV = 128
LAT_DEV = 32
LON_DEV = 128
BLOCK_OBS_SLOTS = 128
BPP = 2
WINDOW_SLOTS = 7
LAT = 128
LONS = 1024
NB = 16
TOTAL_OBS_BLOCKS = 512
N_BAND = 4
N_LON = 8
DEVICES = 32


def touch_ends(drawn, rng, least, largest):
    place = [jax.random.randint(jax.random.fold_in(rng, axis), (), 0, length) for axis, length in enumerate(drawn.shape)]
    widest = drawn.shape.index(max(drawn.shape))
    beside = place[:widest] + [(place[widest] + 1) % drawn.shape[widest]] + place[widest + 1:]
    return drawn.at[tuple(place)].set(least).at[tuple(beside)].set(largest)


def shard_levels(stream_key, extent, cuts, low, largest):
    def one(position, shards_of):
        draws = jax.random.uniform(jax.random.fold_in(jax.random.fold_in(stream_key, 6), position), (shards_of,), jnp.float32, low / len(cuts), largest / len(cuts))
        return jnp.repeat(jnp.exp(draws), extent[position] // shards_of).reshape((-1,) + (1,) * (len(extent) - position - 1))

    loudness = one(*cuts[0])
    for cut in cuts[1:]:
        loudness = loudness * one(*cut)
    return loudness


def gaussian(rng, dims, spread, most, cuts=(), kind=jnp.bfloat16):
    array = jax.random.normal(rng, dims, jnp.float32) * spread
    if len(cuts) > 0:
        array = shard_levels(rng, dims, cuts, -0.22, 0.18) * array
    return jnp.clip(array, min=-most, max=most).astype(kind)


def setup_inputs(seed: int = 0) -> dict:
    keys = jax.random.split(jax.random.key(seed), 11)
    return {
        "latent": gaussian(keys[0], (LAT, LONS, C), 1.0, 6.0, ((0, 4), (1, 8))),
        "row_index": touch_ends(jax.random.randint(keys[1], (N_BAND, N_LON, NB), 0, LAT_DEV), jax.random.fold_in(keys[1], 1), 0, LAT_DEV - 1).astype(jnp.int32),
        "interp_weights": gaussian(keys[2], (TOTAL_OBS_BLOCKS, BLOCK_OBS_SLOTS, LON_DEV), LON_DEV ** -0.5, 0.5, ((0, 32),)),
        "observation_slot_index": touch_ends(jax.random.randint(keys[3], (TOTAL_OBS_BLOCKS, BLOCK_OBS_SLOTS), 0, WINDOW_SLOTS), jax.random.fold_in(keys[3], 1), 0, WINDOW_SLOTS - 1).astype(jnp.int32),
        "counts": touch_ends(jax.random.randint(keys[4], (TOTAL_OBS_BLOCKS,), BLOCK_OBS_SLOTS // 4, BLOCK_OBS_SLOTS + 1), jax.random.fold_in(keys[4], 1), BLOCK_OBS_SLOTS // 4, BLOCK_OBS_SLOTS).astype(jnp.int32),
        "targets": gaussian(keys[5], (TOTAL_OBS_BLOCKS, BLOCK_OBS_SLOTS, NV), 1.0, 6.0, ((0, 32),)),
        "gain": jnp.clip(1.0 + 0.1 * jax.random.normal(keys[6], (C,), jnp.float32), 0.5, 1.5),
        "w_in": gaussian(keys[7], (C, HID), C ** -0.5, 0.375),
        "w_out": gaussian(keys[8], (HID, C), HID ** -0.5, 0.25),
        "head": gaussian(keys[9], (C, NV), C ** -0.5, 0.375),
    }


norm_eps = 1e-05

def rounded_slots(values):
    return lax.optimization_barrier(values.astype(jnp.bfloat16))

def cycle_mix(layer_in):
    return layer_in + 0.5 * (jnp.roll(layer_in, 1, axis=-2) + jnp.roll(layer_in, -1, axis=-2))

def silu_slope(pre_act):
    sigmoid_a = jax.nn.sigmoid(pre_act)
    return sigmoid_a * (1.0 + pre_act * (1.0 - sigmoid_a))

def processor_row(lat_row, gain, w_in, w_out):
    summed = cycle_mix(lat_row.astype(jnp.float32))
    inv_rms = lax.rsqrt(lax.optimization_barrier(jnp.mean(summed * summed, axis=-1, keepdims=True)) + norm_eps)
    normed = (summed * inv_rms * gain).astype(jnp.bfloat16)
    pre_act = jnp.dot(normed, w_in, preferred_element_type=jnp.float32)
    activated = jax.nn.silu(pre_act).astype(jnp.bfloat16)
    advanced = (lat_row.astype(jnp.float32) + jnp.dot(activated, w_out, preferred_element_type=jnp.float32)).astype(jnp.bfloat16)
    return (summed, inv_rms, normed, pre_act, activated, advanced)

def per_device(values):
    return values.reshape((DEVICES, NB) + values.shape[1:])

def reference(latent, row_index, interp_weights, observation_slot_index, counts, targets, gain, w_in, w_out, head):
    channels = latent.shape[-1]

    def forward_row(lat_row):
        return processor_row(lat_row, gain, w_in, w_out)[5]
    advanced = lax.map(forward_row, latent)
    stacked = jnp.concatenate([latent, advanced], axis=-1).reshape(LAT, N_LON, LON_DEV, 2 * channels)
    loss_scale = 1.0 / math.sqrt(BLOCK_OBS_SLOTS)
    block_ids = jnp.arange(NB, dtype=jnp.int32)
    owner_ids = block_ids // BPP
    slot_ids = block_ids % BPP
    live_base = jnp.arange(BLOCK_OBS_SLOTS, dtype=jnp.int32)
    device_ids = jnp.arange(DEVICES, dtype=jnp.int32)

    def obs_device(carry, inputs):
        grid_grad, head_grad = carry
        device, weights_dev, device_slot_count, counts_dev, targets_dev = inputs
        band = device // N_LON
        sender = device % N_LON
        row_ids = row_index[band, owner_ids, sender * BPP + slot_ids].astype(jnp.int32)
        glob_rows = band * LAT_DEV + row_ids
        tile_pairs = stacked[glob_rows, owner_ids].astype(jnp.float32)
        temporal_weight = rounded_slots(device_slot_count.astype(jnp.float32) / (WINDOW_SLOTS - 1)).astype(jnp.float32)[..., None]
        weights_f = weights_dev.astype(jnp.float32)
        proj_old = jnp.einsum('bol,blc->boc', weights_f, tile_pairs[..., :channels])
        proj_new = jnp.einsum('bol,blc->boc', weights_f, tile_pairs[..., channels:])
        obs_latent = ((1.0 - temporal_weight) * proj_old + temporal_weight * proj_new).astype(jnp.bfloat16).reshape(-1, channels)
        predicted = jnp.dot(obs_latent, head, preferred_element_type=jnp.float32)
        live_rows = (live_base[None, :] < counts_dev[:, None]).reshape(-1, 1)
        residual = jnp.where(live_rows, predicted - targets_dev.reshape(-1, predicted.shape[-1]).astype(jnp.float32), 0.0)
        pred_grad = (residual * loss_scale).astype(jnp.bfloat16)
        head_grad = head_grad + jnp.dot(obs_latent.T, pred_grad, preferred_element_type=jnp.float32)
        obs_grad = jnp.dot(pred_grad, head.T, preferred_element_type=jnp.float32)
        obs_grad = rounded_slots(obs_grad).astype(jnp.float32).reshape(NB, BLOCK_OBS_SLOTS, channels)
        back_old = rounded_slots((1.0 - temporal_weight) * obs_grad).astype(jnp.float32)
        back_new = rounded_slots(temporal_weight * obs_grad).astype(jnp.float32)
        tile_old = jnp.einsum('bol,boc->blc', weights_f, back_old)
        tile_new = jnp.einsum('bol,boc->blc', weights_f, back_new)
        tile_grads = rounded_slots(jnp.concatenate([tile_old, tile_new], axis=-1)).astype(jnp.float32)
        grid_grad = grid_grad.at[glob_rows, owner_ids].add(tile_grads)
        return ((grid_grad, head_grad), None)
    start = (jnp.zeros((LAT, N_LON, LON_DEV, 2 * channels), jnp.float32), jnp.zeros(head.shape, jnp.float32))
    (grid_grad, head_grad), _ = lax.scan(obs_device, start, (device_ids, per_device(interp_weights), per_device(observation_slot_index), per_device(counts), per_device(targets)))
    grid_grad = grid_grad.reshape(LAT, LONS, 2 * channels)

    def backward_row(carry, inputs):
        grad_in, grad_out, grad_gain = carry
        lat_row, row_grad = inputs
        summed, inv_rms, normed, pre_act, activated, advanced = processor_row(lat_row, gain, w_in, w_out)
        grad_adv = row_grad[:, channels:].astype(jnp.bfloat16)
        grad_out = grad_out + jnp.dot(activated.T, grad_adv, preferred_element_type=jnp.float32)
        act_grad = jnp.dot(grad_adv, w_out.T, preferred_element_type=jnp.float32)
        pre_grad = (act_grad * silu_slope(pre_act)).astype(jnp.bfloat16)
        grad_in = grad_in + jnp.dot(normed.T, pre_grad, preferred_element_type=jnp.float32)
        normed_grad = jnp.dot(pre_grad, w_in.T, preferred_element_type=jnp.float32)
        grad_gain = grad_gain + lax.optimization_barrier(jnp.sum(normed_grad * summed * inv_rms, axis=0))
        gained = normed_grad * gain
        summed_grad = inv_rms * (gained - summed * inv_rms * inv_rms * lax.optimization_barrier(jnp.mean(gained * summed, axis=-1, keepdims=True)))
        latent_grad = row_grad[:, :channels] + row_grad[:, channels:] + cycle_mix(summed_grad)
        return ((grad_in, grad_out, grad_gain), latent_grad)
    start_back = (jnp.zeros(w_in.shape, jnp.float32), jnp.zeros(w_out.shape, jnp.float32), jnp.zeros(gain.shape, jnp.float32))
    (grad_in, grad_out, grad_gain), grad_latent = lax.scan(backward_row, start_back, (latent, grid_grad))
    return (grad_latent, grad_in / DEVICES, grad_out / DEVICES, grad_gain / DEVICES, head_grad / DEVICES)
```

```python
import functools
import math

import jax
import jax.numpy as jnp
from jax import lax
from jax.experimental import pallas as pl
from jax.experimental.pallas import tpu as pltpu
from jax.sharding import PartitionSpec as P

WINDOW_SLOTS = 7
norm_eps = 1e-05
f32, bf16 = jnp.float32, jnp.bfloat16
MESH = pl.DeviceIdType.MESH


def dot(a, b, dims=((1,), (0,))):
    return lax.dot_general(a, b, (dims, ((), ())), preferred_element_type=f32)


NN = ((1,), (0,))
NT = ((1,), (1,))
TN = ((0,), (0,))


def shifted(x, first, last):
    cells = x.shape[0]
    place = lax.broadcasted_iota(jnp.int32, x.shape, 0)
    before = jnp.where(place == 0, first, pltpu.roll(x, 1, 0))
    after = jnp.where(place == cells - 1, last, pltpu.roll(x, cells - 1, 0))
    return before + after


def layer_kernel(
    peers,
    lat_ref,
    rows_smem,
    rows_ref,
    w_ref,
    t_ref,
    slot_ref,
    count_ref,
    gain_ref,
    w_in_ref,
    w_out_ref,
    head_ref,
    part_ref,
    edge_ref,
    g_in,
    g_out,
    g_gain,
    g_head,
    wbuf,
    tbuf,
    aux,
    auxbuf,
    edge_f,
    edge_send,
    edge_recv,
    sel,
    u_s,
    inv_s,
    normed_s,
    act_s,
    slope_s,
    adv_s,
    sg_edge,
    send_w,
    send_t,
    send_a,
    recv_w,
    recv_t,
    recv_a,
    send_e,
    recv_e,
):
    lat_rows, cells, channels = lat_ref.shape
    blocks, obs = slot_ref.shape
    per = blocks // peers
    me = lax.axis_index("lon")
    right, left = lax.rem(me + 1, peers), lax.rem(me + peers - 1, peers)

    barrier = pltpu.get_barrier_semaphore()
    for d in range(1, peers):
        pl.semaphore_signal(
            barrier, inc=1, device_id={"lon": lax.rem(me + d, peers)}, device_id_type=MESH
        )
    pl.semaphore_wait(barrier, peers - 1)

    def exchange(d):
        to = lax.rem(me + d, peers)
        src, dst = pl.ds(to * per, per), pl.ds(me * per, per)
        copies = []
        for a, b, ss, rs in (
            (w_ref, wbuf, send_w, recv_w),
            (t_ref, tbuf, send_t, recv_t),
            (aux, auxbuf, send_a, recv_a),
        ):
            copies.append(
                pltpu.make_async_remote_copy(
                    src_ref=a.at[src],
                    dst_ref=b.at[dst],
                    send_sem=ss.at[to],
                    recv_sem=rs.at[me],
                    device_id={"lon": to},
                    device_id_type=MESH,
                )
            )
        return copies

    order = [peers // 2]
    for d in range(peers // 2 - 1, 0, -1):
        order += [d, peers - d]
    sends = {d: exchange(d) for d in order}
    for d in order:
        sends[d][0].start()
        sends[d][1].start()
    mine = pl.ds(me * per, per)
    pltpu.make_async_copy(w_ref.at[mine], wbuf.at[mine], recv_w.at[me]).start()
    pltpu.make_async_copy(t_ref.at[mine], tbuf.at[mine], recv_t.at[me]).start()

    coef = (slot_ref[...].astype(f32) / (WINDOW_SLOTS - 1)).astype(bf16).astype(f32)
    live = lax.broadcasted_iota(jnp.int32, (blocks, obs), 1) < count_ref[...]
    coded = jnp.where(live, coef, -1.0)
    aux[...] = jnp.broadcast_to(coded[:, None, :], aux.shape)
    for d in order:
        sends[d][2].start()
    pltpu.make_async_copy(aux.at[mine], auxbuf.at[mine], recv_a.at[me]).start()

    for r in range(lat_rows):
        edge_f[0, r : r + 1, :] = lat_ref[r, cells - 16 : cells, :].astype(f32)[15:16]
        edge_f[1, r : r + 1, :] = lat_ref[r, 0:16, :].astype(f32)[0:1]
    edge_send[0:2] = edge_f[...].astype(bf16)

    def edge_copy(phase, side):
        slot = 2 * phase + side
        return pltpu.make_async_remote_copy(
            src_ref=edge_send.at[slot],
            dst_ref=edge_recv.at[slot],
            send_sem=send_e.at[slot],
            recv_sem=recv_e.at[slot],
            device_id={"lon": left if side else right},
            device_id_type=MESH,
        )

    first_edges = [edge_copy(0, 0), edge_copy(0, 1)]
    for c in first_edges:
        c.start()

    g_in[...] = jnp.zeros_like(g_in)
    g_out[...] = jnp.zeros_like(g_out)
    g_gain[...] = jnp.zeros_like(g_gain)
    g_head[...] = jnp.zeros_like(g_head)
    gain = gain_ref[...]
    onehot = (
        rows_ref[...] == lax.broadcasted_iota(jnp.int32, (blocks, lat_rows), 1)
    ).astype(f32).astype(bf16)

    for c in first_edges:
        c.wait_recv()
    sel[0] = dot(onehot, edge_recv[0])
    sel[1] = dot(onehot, edge_recv[1])

    def forward(j, carry):
        tile = lat_ref[rows_smem[j]]
        x = tile.astype(f32)
        summed = x + 0.5 * shifted(x, sel[0, pl.ds(j, 1), :], sel[1, pl.ds(j, 1), :])
        inv = lax.rsqrt(jnp.mean(summed * summed, axis=-1, keepdims=True) + norm_eps)
        u = summed * inv
        normed = (u * gain).astype(bf16)
        pre = dot(normed, w_in_ref[...])
        sig = jax.nn.sigmoid(pre)
        act = (pre * sig).astype(bf16)
        u_s[j] = u
        inv_s[j] = inv
        normed_s[j] = normed
        act_s[j] = act
        slope_s[j] = sig * (1.0 + pre * (1.0 - sig))
        adv_s[j] = (x + dot(act, w_out_ref[...])).astype(bf16)
        return carry

    lax.fori_loop(0, blocks, forward, 0)

    eye = lax.broadcasted_iota(jnp.int32, (obs, obs), 0) == lax.broadcasted_iota(
        jnp.int32, (obs, obs), 1
    )
    loss_scale = 1.0 / math.sqrt(obs)

    def backward(i, carry):
        odd = lax.rem(i, 2)
        s = lax.rem(me + odd * ((i + 1) // 2) + (1 - odd) * (peers - i // 2), peers)
        base = s * per
        span = pl.ds(base, per)
        for buf, sem in ((wbuf, recv_w), (tbuf, recv_t), (auxbuf, recv_a)):
            pltpu.make_async_copy(buf.at[span], buf.at[span], sem.at[s]).wait()
        codes, lats = [], []
        for k in range(per):
            code = jnp.where(eye, auxbuf[base + k][0:1, :], 0.0)
            code = jnp.sum(code, axis=1, keepdims=True)
            codes.append(code)
            c = jnp.maximum(code, 0.0)
            w = wbuf[base + k]
            old = dot(w, lat_ref[rows_smem[base + k]])
            new = dot(w, adv_s[base + k])
            lats.append(((1.0 - c) * old + c * new).astype(bf16))
        obs_latent = jnp.concatenate(lats, axis=0)
        code = jnp.concatenate(codes, axis=0)
        c = jnp.maximum(code, 0.0)
        head = head_ref[...]
        predicted = dot(obs_latent, head)
        goals = tbuf[span].reshape(per * obs, head.shape[1]).astype(f32)
        residual = jnp.where(code >= 0.0, predicted - goals, 0.0)
        pred_grad = (residual * loss_scale).astype(bf16)
        g_head[...] += dot(obs_latent, pred_grad, TN)
        obs_grad = dot(pred_grad, head, NT).astype(bf16).astype(f32)
        back_old = ((1.0 - c) * obs_grad).astype(bf16)
        back_new = (c * obs_grad).astype(bf16)
        olds, news = [], []
        for k in range(per):
            w = wbuf[base + k]
            sl = slice(k * obs, (k + 1) * obs)
            olds.append(dot(w, back_old[sl], TN).astype(bf16))
            news.append(dot(w, back_new[sl], TN).astype(bf16))
        tile_new = jnp.concatenate(news, axis=0)
        act = act_s[span].reshape(per * cells, -1)
        slope = slope_s[span].reshape(per * cells, -1)
        normed = normed_s[span].reshape(per * cells, channels)
        u = u_s[span].reshape(per * cells, channels)
        g_out[...] += dot(act, tile_new, TN)
        pre_grad = (dot(tile_new, w_out_ref[...], NT) * slope).astype(bf16)
        g_in[...] += dot(normed, pre_grad, TN)
        normed_grad = dot(pre_grad, w_in_ref[...], NT)
        ng_u = normed_grad * u
        g_gain[...] += jnp.sum(ng_u, axis=0, keepdims=True)
        mean = jnp.mean(ng_u * gain, axis=-1, keepdims=True)
        core = normed_grad * gain - u * mean
        for k in range(per):
            sl = slice(k * cells, (k + 1) * cells)
            sg = inv_s[base + k] * core[sl]
            sg_edge[0, pl.ds(base + k, 1), :] = sg[cells - 1 : cells]
            sg_edge[1, pl.ds(base + k, 1), :] = sg[0:1]
            part_ref[base + k] = (
                olds[k].astype(f32) + news[k].astype(f32) + sg + 0.5 * shifted(sg, 0.0, 0.0)
            )
        return carry

    lax.fori_loop(0, peers, backward, 0)

    edge_send[2] = dot(onehot, sg_edge[0].astype(bf16), TN).astype(bf16)
    edge_send[3] = dot(onehot, sg_edge[1].astype(bf16), TN).astype(bf16)
    last_edges = [edge_copy(1, 0), edge_copy(1, 1)]
    for c in last_edges:
        c.start()
    for d in order:
        for c in sends[d]:
            c.wait_send()
    for c in first_edges:
        c.wait_send()
    for c in last_edges:
        c.wait()
    edge_ref[...] = 0.5 * edge_recv[2:4].astype(f32)


def layer(latent, rows, weights, slots, counts, targets, gain, w_in, w_out, head, peers):
    lat_rows, cells, channels = latent.shape
    blocks, obs = slots.shape
    hid = w_in.shape[1]
    values = head.shape[1]
    vmem, anym = pl.BlockSpec(memory_space=pltpu.VMEM), pl.BlockSpec(memory_space=pl.ANY)
    shape = jax.ShapeDtypeStruct
    dma = pltpu.SemaphoreType.DMA
    flops = 2 * blocks * cells * channels * (6 * hid + 4 * obs + 3 * values)
    return pl.pallas_call(
        functools.partial(layer_kernel, peers),
        out_shape=[
            shape((blocks, cells, channels), f32),
            shape((2, lat_rows, channels), f32),
            shape((channels, hid), f32),
            shape((hid, channels), f32),
            shape((1, channels), f32),
            shape((channels, values), f32),
        ],
        in_specs=[vmem, pl.BlockSpec(memory_space=pltpu.SMEM), vmem, anym, anym] + [vmem] * 6,
        out_specs=[vmem] * 6,
        scratch_shapes=[
            pltpu.VMEM((blocks, obs, cells), bf16),
            pltpu.VMEM((blocks, obs, values), bf16),
            pltpu.VMEM((blocks, 8, obs), f32),
            pltpu.VMEM((blocks, 8, obs), f32),
            pltpu.VMEM((2, lat_rows, channels), f32),
            pltpu.VMEM((4, lat_rows, channels), bf16),
            pltpu.VMEM((4, lat_rows, channels), bf16),
            pltpu.VMEM((2, blocks, channels), f32),
            pltpu.VMEM((blocks, cells, channels), f32),
            pltpu.VMEM((blocks, cells, 1), f32),
            pltpu.VMEM((blocks, cells, channels), bf16),
            pltpu.VMEM((blocks, cells, hid), bf16),
            pltpu.VMEM((blocks, cells, hid), f32),
            pltpu.VMEM((blocks, cells, channels), bf16),
            pltpu.VMEM((2, blocks, channels), f32),
        ]
        + [dma((peers,))] * 6
        + [dma((4,))] * 2,
        compiler_params=pltpu.CompilerParams(
            collective_id=0, has_side_effects=True, vmem_limit_bytes=48 * 1024 * 1024
        ),
        cost_estimate=pl.CostEstimate(
            flops=flops, bytes_accessed=10 * 1024 * 1024, transcendentals=blocks * cells * hid
        ),
    )(
        latent,
        rows,
        rows.reshape(blocks, 1),
        weights,
        targets,
        slots,
        counts.reshape(blocks, 1),
        gain.reshape(1, channels),
        w_in,
        w_out,
        head,
    )


def spread_kernel(step, rows_ref, part_ref, edge_ref, out_ref):
    blocks, cells, channels = part_ref.shape
    first = pl.program_id(0) * step
    out_ref[...] = jnp.zeros_like(out_ref)

    def add(j, carry):
        at = rows_ref[j] - first

        @pl.when((at >= 0) & (at < step))
        def _():
            out_ref[at] += part_ref[j]

        return carry

    lax.fori_loop(0, blocks, add, 0)
    for r in range(step):
        out_ref[r, 0:1, :] += edge_ref[0, pl.ds(first + r, 1), :]
        out_ref[r, cells - 1 : cells, :] += edge_ref[1, pl.ds(first + r, 1), :]


def spread(rows, part, edges, lat_rows):
    blocks, cells, channels = part.shape
    step = 4
    vmem = pl.BlockSpec(memory_space=pltpu.VMEM)
    return pl.pallas_call(
        functools.partial(spread_kernel, step),
        out_shape=jax.ShapeDtypeStruct((lat_rows, cells, channels), f32),
        grid=(lat_rows // step,),
        in_specs=[pl.BlockSpec(memory_space=pltpu.SMEM), vmem, vmem],
        out_specs=pl.BlockSpec((step, cells, channels), lambda i: (i, 0, 0)),
        compiler_params=pltpu.CompilerParams(vmem_limit_bytes=32 * 1024 * 1024),
        cost_estimate=pl.CostEstimate(
            flops=blocks * cells * channels,
            bytes_accessed=4 * (blocks + lat_rows) * cells * channels,
            transcendentals=0,
        ),
    )(rows, part, edges)


def body(latent, row_index, weights, slots, counts, targets, gain, w_in, w_out, head):
    peers = lax.axis_size("lon")
    devices_all = lax.axis_size("band") * peers
    rows = row_index.reshape(-1)
    part, edges, g_in, g_out, g_gain, g_head = layer(
        latent, rows, weights, slots, counts, targets, gain, w_in, w_out, head, peers
    )
    grad_latent = spread(rows, part, edges, latent.shape[0])
    totals = lax.psum((g_in, g_out, g_gain.reshape(-1), g_head), ("band", "lon"))
    return (grad_latent,) + tuple(total / devices_all for total in totals)


def solution(mesh):
    return jax.shard_map(
        body,
        mesh=mesh,
        in_specs=(
            P("band", "lon", None),
            P("band", "lon", None),
            P(("band", "lon"), None, None),
            P(("band", "lon"), None),
            P(("band", "lon")),
            P(("band", "lon"), None, None),
            P(),
            P(),
            P(),
            P(),
        ),
        out_specs=(P("band", "lon", None), P(), P(), P(), P()),
        check_vma=False,
    )
```

```python
import functools
import math

import jax
import jax.numpy as jnp
from jax import lax
from jax.experimental import pallas as pl
from jax.experimental.pallas import tpu as pltpu
from jax.sharding import PartitionSpec as P

WINDOW_SLOTS = 7
norm_eps = 1e-05
f32, bf16 = jnp.float32, jnp.bfloat16
MESH = pl.DeviceIdType.MESH


def dot(a, b, dims=((1,), (0,))):
    return lax.dot_general(a, b, (dims, ((), ())), preferred_element_type=f32)


NN = ((1,), (0,))
NT = ((1,), (1,))
TN = ((0,), (0,))


def shifted(x, first, last):
    cells = x.shape[0]
    place = lax.broadcasted_iota(jnp.int32, x.shape, 0)
    before = jnp.where(place == 0, first, pltpu.roll(x, 1, 0))
    after = jnp.where(place == cells - 1, last, pltpu.roll(x, cells - 1, 0))
    return before + after


def layer_kernel(
    peers,
    bands,
    rows_smem,
    count_smem,
    lat_hbm,
    w_ref,
    t_ref,
    slot_hbm,
    gain_hbm,
    w_in_hbm,
    w_out_hbm,
    head_hbm,
    part_ref,
    edge_ref,
    sums_ref,
    lat_ref,
    slot_ref,
    gain_ref,
    w_in_ref,
    w_out_ref,
    head_ref,
    g_in,
    g_out,
    g_gain,
    g_head,
    onehot_f,
    live_f,
    acc,
    from_core,
    core_sum,
    from_band,
    band_sum,
    from_lon,
    total,
    wbuf,
    tbuf,
    aux,
    auxbuf,
    edge_f,
    edge_send,
    edge_recv,
    sel,
    u_s,
    inv_s,
    normed_s,
    act_s,
    slope_s,
    adv_s,
    sg_edge,
    send_w,
    send_t,
    send_a,
    recv_w,
    recv_t,
    recv_a,
    send_e,
    recv_e,
    load_sem,
    core_sems,
    band_sems,
    lon_sems,
):
    lat_rows, cells, channels = lat_ref.shape
    blocks, obs = slot_ref.shape
    per = blocks // peers
    me = lax.axis_index("lon")
    band = lax.axis_index("band")
    right, left = lax.rem(me + 1, peers), lax.rem(me + peers - 1, peers)

    loads = [
        pltpu.make_async_copy(a, b, load_sem.at[i])
        for i, (a, b) in enumerate(
            (
                (slot_hbm, slot_ref),
                (lat_hbm, lat_ref),
                (gain_hbm, gain_ref),
                (w_in_hbm, w_in_ref),
                (w_out_hbm, w_out_ref),
                (head_hbm, head_ref),
            )
        )
    ]
    for load in loads:
        load.start()

    barrier = pltpu.get_barrier_semaphore()
    for d in range(1, peers):
        pl.semaphore_signal(
            barrier, inc=1, device_id={"lon": lax.rem(me + d, peers)}, device_id_type=MESH
        )
    for d in range(1, bands):
        pl.semaphore_signal(
            barrier, inc=1, device_id={"band": lax.rem(band + d, bands)}, device_id_type=MESH
        )
    pl.semaphore_wait(barrier, peers + bands - 2)

    def exchange(d):
        to = lax.rem(me + d, peers)
        src, dst = pl.ds(to * per, per), pl.ds(me * per, per)
        copies = []
        for a, b, ss, rs in (
            (w_ref, wbuf, send_w, recv_w),
            (t_ref, tbuf, send_t, recv_t),
            (aux, auxbuf, send_a, recv_a),
        ):
            copies.append(
                pltpu.make_async_remote_copy(
                    src_ref=a.at[src],
                    dst_ref=b.at[dst],
                    send_sem=ss.at[to],
                    recv_sem=rs.at[me],
                    device_id={"lon": to},
                    device_id_type=MESH,
                )
            )
        return copies

    order = [peers // 2]
    for d in range(peers // 2 - 1, 0, -1):
        order += [d, peers - d]
    sends = {d: exchange(d) for d in order}
    for d in order:
        sends[d][0].start()
        sends[d][1].start()
    mine = pl.ds(me * per, per)
    pltpu.make_async_copy(w_ref.at[mine], wbuf.at[mine], recv_w.at[me]).start()
    pltpu.make_async_copy(t_ref.at[mine], tbuf.at[mine], recv_t.at[me]).start()

    lane = lax.broadcasted_iota(jnp.int32, (1, obs), 1)
    row_lane = lax.broadcasted_iota(jnp.int32, (1, lat_rows), 1)
    for j in range(blocks):
        live_f[j : j + 1, :] = (lane < count_smem[j]).astype(f32)
        onehot_f[j : j + 1, :] = (row_lane == rows_smem[0, 0, j]).astype(f32)
    loads[0].wait()
    coef = (slot_ref[...].astype(f32) / (WINDOW_SLOTS - 1)).astype(bf16).astype(f32)
    coded = jnp.where(live_f[...] > 0.0, coef, -1.0)
    aux[...] = jnp.broadcast_to(coded[:, None, :], aux.shape)
    for d in order:
        sends[d][2].start()
    pltpu.make_async_copy(aux.at[mine], auxbuf.at[mine], recv_a.at[me]).start()

    loads[1].wait()
    for r in range(lat_rows):
        edge_f[0, r : r + 1, :] = lat_ref[r, cells - 16 : cells, :].astype(f32)[15:16]
        edge_f[1, r : r + 1, :] = lat_ref[r, 0:16, :].astype(f32)[0:1]
    edge_send[0:2] = edge_f[...].astype(bf16)

    def edge_copy(phase, side):
        slot = 2 * phase + side
        return pltpu.make_async_remote_copy(
            src_ref=edge_send.at[slot],
            dst_ref=edge_recv.at[slot],
            send_sem=send_e.at[slot],
            recv_sem=recv_e.at[slot],
            device_id={"lon": left if side else right},
            device_id_type=MESH,
        )

    first_edges = [edge_copy(0, 0), edge_copy(0, 1)]
    for c in first_edges:
        c.start()

    g_in[...] = jnp.zeros_like(g_in)
    g_out[...] = jnp.zeros_like(g_out)
    g_gain[...] = jnp.zeros_like(g_gain)
    g_head[...] = jnp.zeros_like(g_head)
    for load in loads[2:]:
        load.wait()
    gain = gain_ref[...]
    onehot = onehot_f[...].astype(bf16)

    for c in first_edges:
        c.wait_recv()
    sel[0] = dot(onehot, edge_recv[0])
    sel[1] = dot(onehot, edge_recv[1])

    group = 2 * per if blocks % (2 * per) == 0 else per

    def forward(i, carry):
        xs, normeds = [], []
        for k in range(group):
            j = i * group + k
            x = lat_ref[rows_smem[0, 0, j]].astype(f32)
            summed = x + 0.5 * shifted(x, sel[0, pl.ds(j, 1), :], sel[1, pl.ds(j, 1), :])
            inv = lax.rsqrt(jnp.mean(summed * summed, axis=-1, keepdims=True) + norm_eps)
            u = summed * inv
            normed = (u * gain).astype(bf16)
            u_s[j] = u
            inv_s[j] = inv
            normed_s[j] = normed
            xs.append(x)
            normeds.append(normed)
        pre = dot(jnp.concatenate(normeds, axis=0), w_in_ref[...])
        sig = jax.nn.sigmoid(pre)
        act = (pre * sig).astype(bf16)
        slope = sig * (1.0 + pre * (1.0 - sig))
        adv = (jnp.concatenate(xs, axis=0) + dot(act, w_out_ref[...])).astype(bf16)
        for k in range(group):
            j, sl = i * group + k, slice(k * cells, (k + 1) * cells)
            act_s[j] = act[sl]
            slope_s[j] = slope[sl]
            adv_s[j] = adv[sl]
        return carry

    lax.fori_loop(0, blocks // group, forward, 0)

    eye = lax.broadcasted_iota(jnp.int32, (obs, obs), 0) == lax.broadcasted_iota(
        jnp.int32, (obs, obs), 1
    )
    loss_scale = 1.0 / math.sqrt(obs)

    def backward(i, carry):
        odd = lax.rem(i, 2)
        s = lax.rem(me + odd * ((i + 1) // 2) + (1 - odd) * (peers - i // 2), peers)
        base = s * per
        span = pl.ds(base, per)
        for buf, sem in ((wbuf, recv_w), (tbuf, recv_t), (auxbuf, recv_a)):
            pltpu.make_async_copy(buf.at[span], buf.at[span], sem.at[s]).wait()
        codes, lats = [], []
        for k in range(per):
            code = jnp.where(eye, auxbuf[base + k][0:1, :], 0.0)
            code = jnp.sum(code, axis=1, keepdims=True)
            codes.append(code)
            c = jnp.maximum(code, 0.0)
            w = wbuf[base + k]
            old = dot(w, lat_ref[rows_smem[0, 0, base + k]])
            new = dot(w, adv_s[base + k])
            lats.append(((1.0 - c) * old + c * new).astype(bf16))
        obs_latent = jnp.concatenate(lats, axis=0)
        code = jnp.concatenate(codes, axis=0)
        c = jnp.maximum(code, 0.0)
        head = head_ref[...]
        predicted = dot(obs_latent, head)
        goals = tbuf[span].reshape(per * obs, head.shape[1]).astype(f32)
        residual = jnp.where(code >= 0.0, predicted - goals, 0.0)
        pred_grad = (residual * loss_scale).astype(bf16)
        g_head[...] += dot(obs_latent, pred_grad, TN)
        obs_grad = dot(pred_grad, head, NT).astype(bf16).astype(f32)
        back_old = ((1.0 - c) * obs_grad).astype(bf16)
        back_new = (c * obs_grad).astype(bf16)
        olds, news = [], []
        for k in range(per):
            w = wbuf[base + k]
            sl = slice(k * obs, (k + 1) * obs)
            olds.append(dot(w, back_old[sl], TN).astype(bf16))
            news.append(dot(w, back_new[sl], TN).astype(bf16))
        tile_new = jnp.concatenate(news, axis=0)
        act = act_s[span].reshape(per * cells, -1)
        slope = slope_s[span].reshape(per * cells, -1)
        normed = normed_s[span].reshape(per * cells, channels)
        u = u_s[span].reshape(per * cells, channels)
        g_out[...] += dot(act, tile_new, TN)
        pre_grad = (dot(tile_new, w_out_ref[...], NT) * slope).astype(bf16)
        g_in[...] += dot(normed, pre_grad, TN)
        normed_grad = dot(pre_grad, w_in_ref[...], NT)
        ng_u = normed_grad * u
        g_gain[...] += jnp.sum(ng_u, axis=0, keepdims=True)
        mean = jnp.mean(ng_u * gain, axis=-1, keepdims=True)
        core = normed_grad * gain - u * mean
        for k in range(per):
            sl = slice(k * cells, (k + 1) * cells)
            sg = inv_s[base + k] * core[sl]
            sg_edge[0, pl.ds(base + k, 1), :] = sg[cells - 1 : cells]
            sg_edge[1, pl.ds(base + k, 1), :] = sg[0:1]
            part_ref[base + k] = (
                olds[k].astype(f32) + news[k].astype(f32) + sg + 0.5 * shifted(sg, 0.0, 0.0)
            )
        return carry

    lax.fori_loop(0, peers, backward, 0)

    edge_send[2] = dot(onehot, sg_edge[0].astype(bf16), TN).astype(bf16)
    edge_send[3] = dot(onehot, sg_edge[1].astype(bf16), TN).astype(bf16)
    last_edges = [edge_copy(1, 0), edge_copy(1, 1)]
    for c in last_edges:
        c.start()

    hid, values = w_in_ref.shape[1], head_ref.shape[1]
    at = 0
    for grad in (g_in, g_out, g_head):
        for first in range(0, grad.shape[1], 128):
            acc[at : at + grad.shape[0], :] = grad[:, first : first + 128].astype(bf16)
            at += grad.shape[0]
    lines = [g_gain[:, i : i + 128] for i in range(0, channels, 128)]
    lines.append(jnp.zeros((16 - len(lines), 128), f32))
    acc[at : at + 16, :] = jnp.concatenate(lines, axis=0).astype(bf16)
    if at + 16 < acc.shape[0]:
        acc[at + 16 :, :] = jnp.zeros((acc.shape[0] - at - 16, 128), bf16)

    core, rank, ranks = lax.rem(me, 2), me // 2, peers // 2
    half = acc.shape[0] // 2
    quarter = half // bands
    piece = quarter // ranks

    def rows_of(start, size):
        return pl.ds(pl.multiple_of(start, 16), size)

    def send(src, dst, sems, slot, to):
        copy = pltpu.make_async_remote_copy(
            src_ref=src,
            dst_ref=dst,
            send_sem=sems.at[0, slot],
            recv_sem=sems.at[1, slot],
            device_id=to,
            device_id_type=MESH,
        )
        copy.start()
        return copy

    def finish(copies):
        for copy in copies:
            copy.wait()

    sibling = {"lon": me + 1 - 2 * core}
    finish([send(acc.at[rows_of((1 - core) * half, half)], from_core, core_sems, 0, sibling)])
    core_sum[...] = (
        acc[rows_of(core * half, half), :].astype(f32) + from_core[...].astype(f32)
    ).astype(bf16)
    copies = []
    for d in range(1, bands):
        to = lax.rem(band + d, bands)
        src = core_sum.at[rows_of(to * quarter, quarter)]
        copies.append(send(src, from_band.at[d - 1], band_sems, d - 1, {"band": to}))
    finish(copies)
    added = core_sum[rows_of(band * quarter, quarter), :].astype(f32)
    for d in range(1, bands):
        added = added + from_band[d - 1].astype(f32)
    band_sum[...] = added.astype(bf16)
    copies = []
    for d in range(1, ranks):
        to = lax.rem(rank + d, ranks)
        src = band_sum.at[rows_of(to * piece, piece)]
        copies.append(send(src, from_lon.at[d - 1], lon_sems, d - 1, {"lon": 2 * to + core}))
    finish(copies)
    added = band_sum[rows_of(rank * piece, piece), :].astype(f32)
    for d in range(1, ranks):
        added = added + from_lon[d - 1].astype(f32)
    lot = core * half + band * quarter
    own = rows_of(lot + rank * piece, piece)
    total[own, :] = added.astype(bf16)
    copies = []
    for d in range(1, ranks):
        to = {"lon": 2 * lax.rem(rank + d, ranks) + core}
        copies.append(send(total.at[own], total.at[own], lon_sems, ranks + d - 2, to))
    finish(copies)
    own = rows_of(lot, quarter)
    copies = []
    for d in range(1, bands):
        to = {"band": lax.rem(band + d, bands)}
        copies.append(send(total.at[own], total.at[own], band_sems, bands + d - 2, to))
    finish(copies)
    own = rows_of(core * half, half)
    finish([send(total.at[own], total.at[own], core_sems, 1, sibling)])
    sums_ref[...] = total[...]

    for d in order:
        for c in sends[d]:
            c.wait_send()
    for c in first_edges:
        c.wait_send()
    for c in last_edges:
        c.wait()
    edge_ref[...] = 0.5 * edge_recv[2:4].astype(f32)


def layer(latent, rows, weights, slots, counts, targets, gain, w_in, w_out, head, peers, bands):
    lat_rows, cells, channels = latent.shape
    blocks, obs = slots.shape
    hid = w_in.shape[1]
    values = head.shape[1]
    vmem, anym = pl.BlockSpec(memory_space=pltpu.VMEM), pl.BlockSpec(memory_space=pl.ANY)
    smem = pl.BlockSpec(memory_space=pltpu.SMEM)
    shape = jax.ShapeDtypeStruct
    dma = pltpu.SemaphoreType.DMA
    flops = 2 * blocks * cells * channels * (6 * hid + 4 * obs + 3 * values)
    packed = channels * (2 * hid + values) // 128 + 16
    pieces = bands * peers
    total = pieces * 16 * pl.cdiv(packed, pieces * 16)
    half, quarter = total // 2, total // 2 // bands
    piece, ranks = total // pieces, peers // 2
    return pl.pallas_call(
        functools.partial(layer_kernel, peers, bands),
        out_shape=[
            shape((blocks, cells, channels), f32),
            shape((2, lat_rows, channels), f32),
            shape((total, 128), bf16),
        ],
        in_specs=[smem] * 2 + [anym] * 8,
        out_specs=[vmem] * 3,
        scratch_shapes=[
            pltpu.VMEM(latent.shape, bf16),
            pltpu.VMEM((blocks, obs), jnp.int32),
            pltpu.VMEM((1, channels), f32),
            pltpu.VMEM(w_in.shape, bf16),
            pltpu.VMEM(w_out.shape, bf16),
            pltpu.VMEM(head.shape, bf16),
            pltpu.VMEM(w_in.shape, f32),
            pltpu.VMEM(w_out.shape, f32),
            pltpu.VMEM((1, channels), f32),
            pltpu.VMEM(head.shape, f32),
            pltpu.VMEM((blocks, lat_rows), f32),
            pltpu.VMEM((blocks, obs), f32),
            pltpu.VMEM((total, 128), bf16),
            pltpu.VMEM((half, 128), bf16),
            pltpu.VMEM((half, 128), bf16),
            pltpu.VMEM((bands - 1, quarter, 128), bf16),
            pltpu.VMEM((quarter, 128), bf16),
            pltpu.VMEM((ranks - 1, piece, 128), bf16),
            pltpu.VMEM((total, 128), bf16),
            pltpu.VMEM((blocks, obs, cells), bf16),
            pltpu.VMEM((blocks, obs, values), bf16),
            pltpu.VMEM((blocks, 8, obs), f32),
            pltpu.VMEM((blocks, 8, obs), f32),
            pltpu.VMEM((2, lat_rows, channels), f32),
            pltpu.VMEM((4, lat_rows, channels), bf16),
            pltpu.VMEM((4, lat_rows, channels), bf16),
            pltpu.VMEM((2, blocks, channels), f32),
            pltpu.VMEM((blocks, cells, channels), f32),
            pltpu.VMEM((blocks, cells, 1), f32),
            pltpu.VMEM((blocks, cells, channels), bf16),
            pltpu.VMEM((blocks, cells, hid), bf16),
            pltpu.VMEM((blocks, cells, hid), f32),
            pltpu.VMEM((blocks, cells, channels), bf16),
            pltpu.VMEM((2, blocks, channels), f32),
        ]
        + [dma((peers,))] * 6
        + [dma((4,))] * 2
        + [dma((6,)), dma((2, 2)), dma((2, 2 * (bands - 1))), dma((2, 2 * (ranks - 1)))],
        compiler_params=pltpu.CompilerParams(
            collective_id=0, has_side_effects=True, vmem_limit_bytes=56 * 1024 * 1024
        ),
        cost_estimate=pl.CostEstimate(
            flops=flops, bytes_accessed=10 * 1024 * 1024, transcendentals=blocks * cells * hid
        ),
    )(
        rows,
        counts,
        latent,
        weights,
        targets,
        slots,
        gain.reshape(1, channels),
        w_in,
        w_out,
        head,
    )


def spread_kernel(
    step, scale, rows_ref, part_ref, edge_ref, sums_ref, out_ref, w_in_g, w_out_g, gain_g, head_g
):
    blocks, cells, channels = part_ref.shape
    first = pl.program_id(0) * step
    out_ref[...] = jnp.zeros_like(out_ref)

    def add(j, carry):
        at = rows_ref[0, 0, j] - first

        @pl.when((at >= 0) & (at < step))
        def _():
            out_ref[at] += part_ref[j]

        return carry

    lax.fori_loop(0, blocks, add, 0)
    for r in range(step):
        out_ref[r, 0:1, :] += edge_ref[0, pl.ds(first + r, 1), :]
        out_ref[r, cells - 1 : cells, :] += edge_ref[1, pl.ds(first + r, 1), :]

    @pl.when(pl.program_id(0) == 0)
    def _():
        at = 0
        for grad in (w_in_g, w_out_g, head_g):
            for lane in range(0, grad.shape[1], 128):
                part = sums_ref[at : at + grad.shape[0], :].astype(f32)
                grad[:, lane : lane + 128] = part * scale
                at += grad.shape[0]
        lines = sums_ref[at : at + 16, :].astype(f32) * scale
        for i in range(channels // 128):
            gain_g[:, i * 128 : (i + 1) * 128] = lines[i : i + 1]


def spread(rows, part, edges, sums, lat_rows, w_in, w_out, head, scale):
    blocks, cells, channels = part.shape
    step = 4
    vmem = pl.BlockSpec(memory_space=pltpu.VMEM)
    shape = jax.ShapeDtypeStruct
    return pl.pallas_call(
        functools.partial(spread_kernel, step, scale),
        out_shape=[
            shape((lat_rows, cells, channels), f32),
            shape(w_in.shape, f32),
            shape(w_out.shape, f32),
            shape((1, channels), f32),
            shape(head.shape, f32),
        ],
        grid=(lat_rows // step,),
        in_specs=[pl.BlockSpec(memory_space=pltpu.SMEM), vmem, vmem, vmem],
        out_specs=[pl.BlockSpec((step, cells, channels), lambda i: (i, 0, 0))] + [vmem] * 4,
        compiler_params=pltpu.CompilerParams(vmem_limit_bytes=32 * 1024 * 1024),
        cost_estimate=pl.CostEstimate(
            flops=blocks * cells * channels,
            bytes_accessed=4 * (blocks + lat_rows) * cells * channels,
            transcendentals=0,
        ),
    )(rows, part, edges, sums)


def body(latent, row_index, weights, slots, counts, targets, gain, w_in, w_out, head):
    peers, bands = lax.axis_size("lon"), lax.axis_size("band")
    part, edges, sums = layer(
        latent, row_index, weights, slots, counts, targets, gain, w_in, w_out, head, peers, bands
    )
    grad_latent, g_in, g_out, g_gain, g_head = spread(
        row_index, part, edges, sums, latent.shape[0], w_in, w_out, head, 1.0 / (peers * bands)
    )
    return grad_latent, g_in, g_out, g_gain.reshape(-1), g_head


def solution(mesh):
    return jax.shard_map(
        body,
        mesh=mesh,
        in_specs=(
            P("band", "lon", None),
            P("band", "lon", None),
            P(("band", "lon"), None, None),
            P(("band", "lon"), None),
            P(("band", "lon")),
            P(("band", "lon"), None, None),
            P(),
            P(),
            P(),
            P(),
        ),
        out_specs=(P("band", "lon", None), P(), P(), P(), P()),
        check_vma=False,
    )
```

```python
import functools
import math

import jax
import jax.numpy as jnp
from jax import lax
from jax.experimental import pallas as pl
from jax.experimental.pallas import tpu as pltpu
from jax.sharding import PartitionSpec as P

WINDOW_SLOTS = 7
norm_eps = 1e-05
f32, bf16 = jnp.float32, jnp.bfloat16
MESH = pl.DeviceIdType.MESH


def dot(a, b, dims=((1,), (0,))):
    return lax.dot_general(a, b, (dims, ((), ())), preferred_element_type=f32)


NN = ((1,), (0,))
NT = ((1,), (1,))
TN = ((0,), (0,))


def shifted(x, first, last):
    cells = x.shape[0]
    place = lax.broadcasted_iota(jnp.int32, x.shape, 0)
    before = jnp.where(place == 0, first, pltpu.roll(x, 1, 0))
    after = jnp.where(place == cells - 1, last, pltpu.roll(x, cells - 1, 0))
    return before + after


def layer_kernel(
    peers,
    bands,
    rows_smem,
    count_smem,
    lat_hbm,
    w_ref,
    t_ref,
    slot_hbm,
    gain_hbm,
    w_in_hbm,
    w_out_hbm,
    head_hbm,
    rows_out,
    sums_ref,
    part_ref,
    lat_out,
    lat_ref,
    slot_ref,
    gain_ref,
    w_in_ref,
    w_out_ref,
    head_ref,
    g_in,
    g_out,
    g_gain,
    g_head,
    onehot_f,
    live_f,
    chunk_a,
    chunk_b,
    wbuf,
    tbuf,
    aux,
    auxbuf,
    edge_f,
    edge_send,
    edge_recv,
    sel,
    u_s,
    inv_s,
    normed_s,
    act_s,
    slope_s,
    adv_s,
    sg_edge,
    send_w,
    send_t,
    send_a,
    recv_w,
    recv_t,
    recv_a,
    send_e,
    recv_e,
    load_sem,
    store_sem,
    core_sems,
    band_sems,
    lon_sems,
):
    lat_rows, cells, channels = lat_ref.shape
    blocks, obs = slot_ref.shape
    per = blocks // peers
    me = lax.axis_index("lon")
    band = lax.axis_index("band")
    right, left = lax.rem(me + 1, peers), lax.rem(me + peers - 1, peers)

    def partner(m):
        other, bit = me, 1
        while bit < peers:
            flip = (m // bit) % 2
            other = other + flip * bit * (1 - 2 * ((me // bit) % 2))
            bit *= 2
        return other

    loads = [
        pltpu.make_async_copy(a, b, load_sem.at[i])
        for i, (a, b) in enumerate(
            (
                (slot_hbm, slot_ref),
                (lat_hbm, lat_ref),
                (gain_hbm, gain_ref),
                (w_in_hbm, w_in_ref),
                (w_out_hbm, w_out_ref),
                (head_hbm, head_ref),
            )
        )
    ]
    for load in loads:
        load.start()

    lane = lax.broadcasted_iota(jnp.int32, (1, obs), 1)
    row_lane = lax.broadcasted_iota(jnp.int32, (1, lat_rows), 1)
    for j in range(blocks):
        live_f[j : j + 1, :] = (lane < count_smem[j]).astype(f32)
        onehot_f[j : j + 1, :] = (row_lane == rows_smem[0, 0, j]).astype(f32)
    loads[0].wait()
    coef = (slot_ref[...].astype(f32) / (WINDOW_SLOTS - 1)).astype(bf16).astype(f32)
    coded = jnp.where(live_f[...] > 0.0, coef, -1.0)
    aux[...] = jnp.broadcast_to(coded[:, None, :], aux.shape)
    loads[1].wait()
    for r in range(lat_rows):
        edge_f[0, r : r + 1, :] = lat_ref[r, cells - 16 : cells, :].astype(f32)[15:16]
        edge_f[1, r : r + 1, :] = lat_ref[r, 0:16, :].astype(f32)[0:1]
    edge_send[0:2] = edge_f[...].astype(bf16)

    barrier = pltpu.get_barrier_semaphore()
    for d in range(1, peers):
        pl.semaphore_signal(
            barrier, inc=1, device_id={"lon": lax.rem(me + d, peers)}, device_id_type=MESH
        )
    for d in range(1, bands):
        pl.semaphore_signal(
            barrier, inc=1, device_id={"band": lax.rem(band + d, bands)}, device_id_type=MESH
        )
    pl.semaphore_wait(barrier, peers + bands - 2)

    def edge_copy(phase, side):
        slot = 2 * phase + side
        return pltpu.make_async_remote_copy(
            src_ref=edge_send.at[slot],
            dst_ref=edge_recv.at[slot],
            send_sem=send_e.at[slot],
            recv_sem=recv_e.at[slot],
            device_id={"lon": left if side else right},
            device_id_type=MESH,
        )

    first_edges = [edge_copy(0, 0), edge_copy(0, 1)]
    for c in first_edges:
        c.start()

    def exchange(m):
        to = partner(m)
        src, dst = pl.ds(to * per, per), pl.ds(me * per, per)
        return [
            pltpu.make_async_remote_copy(
                src_ref=a.at[src],
                dst_ref=b.at[dst],
                send_sem=ss.at[to],
                recv_sem=rs.at[me],
                device_id={"lon": to},
                device_id_type=MESH,
            )
            for a, b, ss, rs in (
                (aux, auxbuf, send_a, recv_a),
                (w_ref, wbuf, send_w, recv_w),
                (t_ref, tbuf, send_t, recv_t),
            )
        ]

    sends = [None] + [exchange(m) for m in range(1, peers)]
    for m in range(1, peers):
        sends[m][0].start()
    mine = pl.ds(me * per, per)
    pltpu.make_async_copy(aux.at[mine], auxbuf.at[mine], recv_a.at[me]).start()
    pltpu.make_async_copy(w_ref.at[mine], wbuf.at[mine], recv_w.at[me]).start()
    pltpu.make_async_copy(t_ref.at[mine], tbuf.at[mine], recv_t.at[me]).start()
    far = list(range(peers // 2, peers - 1))
    order = [1]
    for m in range(2, peers // 2):
        order += [far.pop(0), m]
    for m in order + far:
        sends[m][1].start()
        sends[m][2].start()

    g_in[...] = jnp.zeros_like(g_in)
    g_out[...] = jnp.zeros_like(g_out)
    g_gain[...] = jnp.zeros_like(g_gain)
    g_head[...] = jnp.zeros_like(g_head)
    for load in loads[2:]:
        load.wait()
    gain = gain_ref[...]
    onehot = onehot_f[...].astype(bf16)

    for c in first_edges:
        c.wait_recv()
    sel[0] = dot(onehot, edge_recv[0])
    sel[1] = dot(onehot, edge_recv[1])

    group = 2 * per if blocks % (2 * per) == 0 else per

    def forward(i, carry):
        xs, normeds = [], []
        for k in range(group):
            j = i * group + k
            x = lat_ref[rows_smem[0, 0, j]].astype(f32)
            summed = x + 0.5 * shifted(x, sel[0, pl.ds(j, 1), :], sel[1, pl.ds(j, 1), :])
            inv = lax.rsqrt(jnp.mean(summed * summed, axis=-1, keepdims=True) + norm_eps)
            u = summed * inv
            normed = (u * gain).astype(bf16)
            u_s[j] = u
            inv_s[j] = inv
            normed_s[j] = normed
            xs.append(x)
            normeds.append(normed)
        pre = dot(jnp.concatenate(normeds, axis=0), w_in_ref[...])
        sig = jax.nn.sigmoid(pre)
        act = (pre * sig).astype(bf16)
        slope = sig * (1.0 + pre * (1.0 - sig))
        adv = (jnp.concatenate(xs, axis=0) + dot(act, w_out_ref[...])).astype(bf16)
        for k in range(group):
            j, sl = i * group + k, slice(k * cells, (k + 1) * cells)
            act_s[j] = act[sl]
            slope_s[j] = slope[sl]
            adv_s[j] = adv[sl]
        return carry

    lax.fori_loop(0, blocks // group, forward, 0)

    eye = lax.broadcasted_iota(jnp.int32, (obs, obs), 0) == lax.broadcasted_iota(
        jnp.int32, (obs, obs), 1
    )
    loss_scale = 1.0 / math.sqrt(obs)

    def backward(i, carry):
        s, bit = me, 1
        while bit < peers:
            s = s + lax.rem(i // bit, 2) * bit * (1 - 2 * ((me // bit) % 2))
            bit *= 2

        @pl.when(i == peers // 2 - 2)
        def _():
            sends[peers - 1][1].start()
            sends[peers - 1][2].start()

        base = s * per
        span = pl.ds(base, per)
        for buf, sem in ((wbuf, recv_w), (tbuf, recv_t), (auxbuf, recv_a)):
            pltpu.make_async_copy(buf.at[span], buf.at[span], sem.at[s]).wait()
        codes, lats = [], []
        for k in range(per):
            code = jnp.where(eye, auxbuf[base + k][0:1, :], 0.0)
            code = jnp.sum(code, axis=1, keepdims=True)
            codes.append(code)
            c = jnp.maximum(code, 0.0)
            w = wbuf[base + k]
            old = dot(w, lat_ref[rows_smem[0, 0, base + k]])
            new = dot(w, adv_s[base + k])
            lats.append(((1.0 - c) * old + c * new).astype(bf16))
        obs_latent = jnp.concatenate(lats, axis=0)
        code = jnp.concatenate(codes, axis=0)
        c = jnp.maximum(code, 0.0)
        head = head_ref[...]
        predicted = dot(obs_latent, head)
        goals = tbuf[span].reshape(per * obs, head.shape[1]).astype(f32)
        residual = jnp.where(code >= 0.0, predicted - goals, 0.0)
        pred_grad = (residual * loss_scale).astype(bf16)
        g_head[...] += dot(obs_latent, pred_grad, TN)
        obs_grad = dot(pred_grad, head, NT).astype(bf16).astype(f32)
        back_old = ((1.0 - c) * obs_grad).astype(bf16)
        back_new = (c * obs_grad).astype(bf16)
        olds, news = [], []
        for k in range(per):
            w = wbuf[base + k]
            sl = slice(k * obs, (k + 1) * obs)
            olds.append(dot(w, back_old[sl], TN).astype(bf16))
            news.append(dot(w, back_new[sl], TN).astype(bf16))
        tile_new = jnp.concatenate(news, axis=0)
        act = act_s[span].reshape(per * cells, -1)
        slope = slope_s[span].reshape(per * cells, -1)
        normed = normed_s[span].reshape(per * cells, channels)
        u = u_s[span].reshape(per * cells, channels)
        g_out[...] += dot(act, tile_new, TN)
        pre_grad = (dot(tile_new, w_out_ref[...], NT) * slope).astype(bf16)
        g_in[...] += dot(normed, pre_grad, TN)
        normed_grad = dot(pre_grad, w_in_ref[...], NT)
        ng_u = normed_grad * u
        g_gain[...] += jnp.sum(ng_u, axis=0, keepdims=True)
        mean = jnp.mean(ng_u * gain, axis=-1, keepdims=True)
        core = normed_grad * gain - u * mean
        for k in range(per):
            sl = slice(k * cells, (k + 1) * cells)
            sg = inv_s[base + k] * core[sl]
            sg_edge[0, pl.ds(base + k, 1), :] = sg[cells - 1 : cells]
            sg_edge[1, pl.ds(base + k, 1), :] = sg[0:1]
            part_ref[base + k] = (
                olds[k].astype(f32) + news[k].astype(f32) + sg + 0.5 * shifted(sg, 0.0, 0.0)
            )
        return carry

    lax.fori_loop(0, peers, backward, 0)

    edge_send[2] = dot(onehot, sg_edge[0].astype(bf16), TN).astype(bf16)
    edge_send[3] = dot(onehot, sg_edge[1].astype(bf16), TN).astype(bf16)
    last_edges = [edge_copy(1, 0), edge_copy(1, 1)]
    for c in last_edges:
        c.start()


    def pack(acc, grads, tail):
        at = 0
        for grad in grads:
            for first in range(0, grad.shape[1], 128):
                acc[at : at + grad.shape[0], :] = grad[:, first : first + 128].astype(bf16)
                at += grad.shape[0]
        if tail:
            lines = [g_gain[:, i : i + 128] for i in range(0, channels, 128)]
            lines.append(jnp.zeros((16 - len(lines), 128), f32))
            acc[at : at + 16, :] = jnp.concatenate(lines, axis=0).astype(bf16)
            at += 16
        if at < acc.shape[0]:
            acc[at:, :] = jnp.zeros((acc.shape[0] - at, 128), bf16)

    core, rank, ranks = lax.rem(me, 2), me // 2, peers // 2
    sibling = {"lon": me + 1 - 2 * core}
    band_to = [{"band": lax.rem(band + d, bands)} for d in range(1, bands)]
    rank_to = [{"lon": 2 * lax.rem(rank + d, ranks) + core} for d in range(1, ranks)]
    started = []

    def rows_of(start, size):
        return pl.ds(pl.multiple_of(start, 16), size)

    def send(src, dst, sems, chunk, slot, to):
        copy = pltpu.make_async_remote_copy(
            src_ref=src,
            dst_ref=dst,
            send_sem=sems.at[chunk, 0, slot],
            recv_sem=sems.at[chunk, 1, slot],
            device_id=to,
            device_id_type=MESH,
        )
        copy.start()
        started.append(copy)
        return copy

    def arrived(copies):
        for copy in copies:
            copy.wait_recv()

    def reduce_steps(n, chunk):
        acc, from_core, core_sum, from_band, band_sum, from_lon, total = chunk
        half = acc.shape[0] // 2
        quarter = half // bands
        piece = quarter // ranks
        lot = core * half + band * quarter
        got = [send(acc.at[rows_of((1 - core) * half, half)], from_core, core_sems, n, 0, sibling)]
        yield
        arrived(got)
        core_sum[...] = (
            acc[rows_of(core * half, half), :].astype(f32) + from_core[...].astype(f32)
        ).astype(bf16)
        got = []
        for d in range(1, bands):
            src = core_sum.at[rows_of(lax.rem(band + d, bands) * quarter, quarter)]
            got.append(send(src, from_band.at[d - 1], band_sems, n, d - 1, band_to[d - 1]))
        yield
        arrived(got)
        added = core_sum[rows_of(band * quarter, quarter), :].astype(f32)
        for d in range(1, bands):
            added = added + from_band[d - 1].astype(f32)
        band_sum[...] = added.astype(bf16)
        got = []
        for d in range(1, ranks):
            src = band_sum.at[rows_of(lax.rem(rank + d, ranks) * piece, piece)]
            got.append(send(src, from_lon.at[d - 1], lon_sems, n, d - 1, rank_to[d - 1]))
        yield
        arrived(got)
        added = band_sum[rows_of(rank * piece, piece), :].astype(f32)
        for d in range(1, ranks):
            added = added + from_lon[d - 1].astype(f32)
        own = rows_of(lot + rank * piece, piece)
        total[own, :] = added.astype(bf16)
        own = total.at[own]
        got = []
        for d in range(1, ranks):
            got.append(send(own, own, lon_sems, n, ranks + d - 2, rank_to[d - 1]))
        yield
        arrived(got)
        own = total.at[rows_of(lot, quarter)]
        got = []
        for d in range(1, bands):
            got.append(send(own, own, band_sems, n, bands + d - 2, band_to[d - 1]))
        yield
        arrived(got)
        own = total.at[rows_of(core * half, half)]
        got = [send(own, own, core_sems, n, 1, sibling)]
        yield
        arrived(got)
        yield

    pack(chunk_a[0], (g_out,), False)
    steps_a = reduce_steps(0, chunk_a)
    next(steps_a)
    pack(chunk_b[0], (g_in, g_head), True)
    steps_b = reduce_steps(1, chunk_b)
    next(steps_b)

    part_ref[blocks] = jnp.zeros((cells, channels), f32)

    def merge(i, carry):
        j = blocks - 1 - i
        row, later = rows_smem[0, 0, j], blocks
        for other in range(blocks - 1, 0, -1):
            same = (rows_smem[0, 0, other] == row) & (other > j)
            later = jnp.where(same, other, later)
        part_ref[j] = part_ref[j] + part_ref[later]
        return carry

    lax.fori_loop(0, blocks, merge, 0)
    next(steps_a)
    next(steps_b)
    for c in last_edges:
        c.wait_recv()
    edge_f[...] = 0.5 * edge_recv[2:4].astype(f32)

    def gather(r, carry):
        found = blocks
        for j in range(blocks - 1, -1, -1):
            found = jnp.where(rows_smem[0, 0, j] == r, j, found)
        lat_out[r] = part_ref[found]
        lat_out[r, 0:1, :] += edge_f[0, pl.ds(r, 1), :]
        lat_out[r, cells - 1 : cells, :] += edge_f[1, pl.ds(r, 1), :]
        return carry

    lax.fori_loop(0, lat_rows, gather, 0)
    store = pltpu.make_async_copy(lat_out, rows_out, store_sem)
    store.start()
    for _ in range(5):
        next(steps_a)
        next(steps_b)
    split = chunk_a[0].shape[0]
    sums_ref[0:split, :] = chunk_a[-1][...]
    sums_ref[split:, :] = chunk_b[-1][...]

    for copy in started + first_edges + last_edges:
        copy.wait_send()
    for m in range(1, peers):
        for copy in sends[m]:
            copy.wait_send()
    store.wait()


def layer(latent, rows, weights, slots, counts, targets, gain, w_in, w_out, head, peers, bands):
    lat_rows, cells, channels = latent.shape
    blocks, obs = slots.shape
    hid = w_in.shape[1]
    values = head.shape[1]
    vmem, anym = pl.BlockSpec(memory_space=pltpu.VMEM), pl.BlockSpec(memory_space=pl.ANY)
    smem = pl.BlockSpec(memory_space=pltpu.SMEM)
    shape = jax.ShapeDtypeStruct
    dma = pltpu.SemaphoreType.DMA
    flops = 2 * blocks * cells * channels * (6 * hid + 4 * obs + 3 * values)
    pieces, ranks = bands * peers, peers // 2

    def chunk(lines):
        total = pieces * 16 * pl.cdiv(lines, pieces * 16)
        half, quarter, piece = total // 2, total // 2 // bands, total // pieces
        shapes = [
            (total, 128),
            (half, 128),
            (half, 128),
            (bands - 1, quarter, 128),
            (quarter, 128),
            (ranks - 1, piece, 128),
            (total, 128),
        ]
        return total, tuple(pltpu.VMEM(one, bf16) for one in shapes)

    total_a, chunk_a = chunk(channels * hid // 128)
    total_b, chunk_b = chunk(channels * (hid + values) // 128 + 16)
    return pl.pallas_call(
        functools.partial(layer_kernel, peers, bands),
        out_shape=[
            shape((lat_rows, cells, channels), f32),
            shape((total_a + total_b, 128), bf16),
        ],
        in_specs=[smem] * 2 + [anym] * 8,
        out_specs=[anym, vmem],
        scratch_shapes=[
            pltpu.VMEM((blocks + 1, cells, channels), f32),
            pltpu.VMEM((lat_rows, cells, channels), f32),
            pltpu.VMEM(latent.shape, bf16),
            pltpu.VMEM((blocks, obs), jnp.int32),
            pltpu.VMEM((1, channels), f32),
            pltpu.VMEM(w_in.shape, bf16),
            pltpu.VMEM(w_out.shape, bf16),
            pltpu.VMEM(head.shape, bf16),
            pltpu.VMEM(w_in.shape, f32),
            pltpu.VMEM(w_out.shape, f32),
            pltpu.VMEM((1, channels), f32),
            pltpu.VMEM(head.shape, f32),
            pltpu.VMEM((blocks, lat_rows), f32),
            pltpu.VMEM((blocks, obs), f32),
            chunk_a,
            chunk_b,
            pltpu.VMEM((blocks, obs, cells), bf16),
            pltpu.VMEM((blocks, obs, values), bf16),
            pltpu.VMEM((blocks, 8, obs), f32),
            pltpu.VMEM((blocks, 8, obs), f32),
            pltpu.VMEM((2, lat_rows, channels), f32),
            pltpu.VMEM((4, lat_rows, channels), bf16),
            pltpu.VMEM((4, lat_rows, channels), bf16),
            pltpu.VMEM((2, blocks, channels), f32),
            pltpu.VMEM((blocks, cells, channels), f32),
            pltpu.VMEM((blocks, cells, 1), f32),
            pltpu.VMEM((blocks, cells, channels), bf16),
            pltpu.VMEM((blocks, cells, hid), bf16),
            pltpu.VMEM((blocks, cells, hid), f32),
            pltpu.VMEM((blocks, cells, channels), bf16),
            pltpu.VMEM((2, blocks, channels), f32),
        ]
        + [dma((peers,))] * 6
        + [dma((4,))] * 2
        + [dma((6,)), dma(()), dma((2, 2, 2))]
        + [dma((2, 2, 2 * (bands - 1))), dma((2, 2, 2 * (ranks - 1)))],
        compiler_params=pltpu.CompilerParams(
            collective_id=0, has_side_effects=True, vmem_limit_bytes=56 * 1024 * 1024
        ),
        cost_estimate=pl.CostEstimate(
            flops=flops, bytes_accessed=10 * 1024 * 1024, transcendentals=blocks * cells * hid
        ),
    )(
        rows,
        counts,
        latent,
        weights,
        targets,
        slots,
        gain.reshape(1, channels),
        w_in,
        w_out,
        head,
    )


def finish_kernel(
    scale, split, rows_ref, sums_hbm, out_ref, w_in_g, w_out_g, gain_g, head_g, held, sums_ref, sems
):
    count = sems.shape[1] - 1
    size = rows_ref.shape[0] // count
    load = pltpu.make_async_copy(sums_hbm, sums_ref, sems.at[0, count])
    load.start()
    reads, writes = [], []
    for i in range(count):
        part = pl.ds(i * size, size)
        reads.append(pltpu.make_async_copy(rows_ref.at[part], held.at[part], sems.at[0, i]))
        writes.append(pltpu.make_async_copy(held.at[part], out_ref.at[part], sems.at[1, i]))
        reads[-1].start()
    for i in range(count):
        reads[i].wait()
        writes[i].start()
    load.wait()
    at = 0
    for grad in (w_out_g, w_in_g, head_g):
        for lane in range(0, grad.shape[1], 128):
            part = sums_ref[at : at + grad.shape[0], :].astype(f32)
            grad[:, lane : lane + 128] = part * scale
            at += grad.shape[0]
        if grad is w_out_g:
            at = split
    lines = sums_ref[at : at + 16, :].astype(f32) * scale
    for i in range(gain_g.shape[1] // 128):
        gain_g[:, i * 128 : (i + 1) * 128] = lines[i : i + 1]
    for write in writes:
        write.wait()


def finish(rows, sums, w_in, w_out, head, scale, split):
    channels = rows.shape[2]
    vmem, anym = pl.BlockSpec(memory_space=pltpu.VMEM), pl.BlockSpec(memory_space=pl.ANY)
    shape = jax.ShapeDtypeStruct
    return pl.pallas_call(
        functools.partial(finish_kernel, scale, split),
        out_shape=[
            shape(rows.shape, f32),
            shape(w_in.shape, f32),
            shape(w_out.shape, f32),
            shape((1, channels), f32),
            shape(head.shape, f32),
        ],
        in_specs=[anym] * 2,
        out_specs=[anym] + [vmem] * 4,
        scratch_shapes=[
            pltpu.VMEM(rows.shape, f32),
            pltpu.VMEM(sums.shape, bf16),
            pltpu.SemaphoreType.DMA((2, 9)),
        ],
        compiler_params=pltpu.CompilerParams(vmem_limit_bytes=56 * 1024 * 1024),
        cost_estimate=pl.CostEstimate(
            flops=sums.size, bytes_accessed=8 * rows.size + 6 * sums.size, transcendentals=0
        ),
    )(rows, sums)


def body(latent, row_index, weights, slots, counts, targets, gain, w_in, w_out, head):
    peers, bands = lax.axis_size("lon"), lax.axis_size("band")
    split = 16 * bands * peers
    split = split * pl.cdiv(w_in.size // 128, split)
    rows, sums = layer(
        latent, row_index, weights, slots, counts, targets, gain, w_in, w_out, head, peers, bands
    )
    grad_latent, g_in, g_out, g_gain, g_head = finish(
        rows, sums, w_in, w_out, head, 1.0 / (peers * bands), split
    )
    return grad_latent, g_in, g_out, g_gain.reshape(-1), g_head


def solution(mesh):
    return jax.shard_map(
        body,
        mesh=mesh,
        in_specs=(
            P("band", "lon", None),
            P("band", "lon", None),
            P(("band", "lon"), None, None),
            P(("band", "lon"), None),
            P(("band", "lon")),
            P(("band", "lon"), None, None),
            P(),
            P(),
            P(),
            P(),
        ),
        out_specs=(P("band", "lon", None), P(), P(), P(), P()),
        check_vma=False,
    )
```

```python
import functools
import math

import jax
import jax.numpy as jnp
from jax import lax
from jax.experimental import pallas as pl
from jax.experimental.pallas import tpu as pltpu
from jax.sharding import PartitionSpec as P

WINDOW_SLOTS = 7
norm_eps = 1e-05
f32, bf16 = jnp.float32, jnp.bfloat16
MESH = pl.DeviceIdType.MESH


def dot(a, b, dims=((1,), (0,))):
    return lax.dot_general(a, b, (dims, ((), ())), preferred_element_type=f32)


NN = ((1,), (0,))
NT = ((1,), (1,))
TN = ((0,), (0,))


def shifted(x, first, last):
    cells = x.shape[0]
    place = lax.broadcasted_iota(jnp.int32, x.shape, 0)
    before = jnp.where(place == 0, first, pltpu.roll(x, 1, 0))
    after = jnp.where(place == cells - 1, last, pltpu.roll(x, cells - 1, 0))
    return before + after


def layer_kernel(
    peers,
    bands,
    rows_smem,
    count_smem,
    lat_hbm,
    w_ref,
    t_ref,
    slot_hbm,
    gain_hbm,
    w_in_hbm,
    w_out_hbm,
    head_hbm,
    rows_out,
    sums_ref,
    part_ref,
    lat_out,
    lat_ref,
    slot_ref,
    gain_ref,
    w_in_ref,
    w_out_ref,
    head_ref,
    g_in,
    g_out,
    g_gain,
    g_head,
    onehot_f,
    live_f,
    chunk_a,
    chunk_b,
    wbuf,
    tbuf,
    aux,
    auxbuf,
    edge_f,
    edge_send,
    edge_recv,
    sel,
    u_s,
    inv_s,
    normed_s,
    act_s,
    slope_s,
    pair_s,
    sg_edge,
    send_w,
    send_t,
    send_a,
    recv_w,
    recv_t,
    recv_a,
    send_e,
    recv_e,
    load_sem,
    store_sem,
    core_sems,
    band_sems,
    lon_sems,
):
    lat_rows, cells, channels = lat_ref.shape
    blocks, obs = slot_ref.shape
    per = blocks // peers
    me = lax.axis_index("lon")
    band = lax.axis_index("band")
    right, left = lax.rem(me + 1, peers), lax.rem(me + peers - 1, peers)

    def partner(m):
        other, bit = me, 1
        while bit < peers:
            flip = (m // bit) % 2
            other = other + flip * bit * (1 - 2 * ((me // bit) % 2))
            bit *= 2
        return other

    loads = [
        pltpu.make_async_copy(a, b, load_sem.at[i])
        for i, (a, b) in enumerate(
            (
                (slot_hbm, slot_ref),
                (lat_hbm, lat_ref),
                (gain_hbm, gain_ref),
                (w_in_hbm, w_in_ref),
                (w_out_hbm, w_out_ref),
                (head_hbm, head_ref),
            )
        )
    ]
    for load in loads:
        load.start()

    lane = lax.broadcasted_iota(jnp.int32, (1, obs), 1)
    row_lane = lax.broadcasted_iota(jnp.int32, (1, lat_rows), 1)
    for j in range(blocks):
        live_f[j : j + 1, :] = (lane < count_smem[j]).astype(f32)
        onehot_f[j : j + 1, :] = (row_lane == rows_smem[0, 0, j]).astype(f32)
    loads[0].wait()
    coef = (slot_ref[...].astype(f32) / (WINDOW_SLOTS - 1)).astype(bf16).astype(f32)
    coded = jnp.where(live_f[...] > 0.0, coef, -1.0)
    aux[...] = jnp.broadcast_to(coded[:, None, :], aux.shape)
    loads[1].wait()
    for r in range(lat_rows):
        edge_f[0, r : r + 1, :] = lat_ref[r, cells - 16 : cells, :].astype(f32)[15:16]
        edge_f[1, r : r + 1, :] = lat_ref[r, 0:16, :].astype(f32)[0:1]
    edge_send[0:2] = edge_f[...].astype(bf16)

    barrier = pltpu.get_barrier_semaphore()
    for d in range(1, peers):
        pl.semaphore_signal(
            barrier, inc=1, device_id={"lon": lax.rem(me + d, peers)}, device_id_type=MESH
        )
    for d in range(1, bands):
        pl.semaphore_signal(
            barrier, inc=1, device_id={"band": lax.rem(band + d, bands)}, device_id_type=MESH
        )
    pl.semaphore_wait(barrier, peers + bands - 2)

    def edge_copy(phase, side):
        slot = 2 * phase + side
        return pltpu.make_async_remote_copy(
            src_ref=edge_send.at[slot],
            dst_ref=edge_recv.at[slot],
            send_sem=send_e.at[slot],
            recv_sem=recv_e.at[slot],
            device_id={"lon": left if side else right},
            device_id_type=MESH,
        )

    first_edges = [edge_copy(0, 0), edge_copy(0, 1)]
    for c in first_edges:
        c.start()

    def exchange(m):
        to = partner(m)
        src, dst = pl.ds(to * per, per), pl.ds(me * per, per)
        return [
            pltpu.make_async_remote_copy(
                src_ref=a.at[src],
                dst_ref=b.at[dst],
                send_sem=ss.at[to],
                recv_sem=rs.at[me],
                device_id={"lon": to},
                device_id_type=MESH,
            )
            for a, b, ss, rs in (
                (aux, auxbuf, send_a, recv_a),
                (w_ref, wbuf, send_w, recv_w),
                (t_ref, tbuf, send_t, recv_t),
            )
        ]

    sends = [None] + [exchange(m) for m in range(1, peers)]
    for m in range(1, peers):
        sends[m][0].start()
    mine = pl.ds(me * per, per)
    pltpu.make_async_copy(aux.at[mine], auxbuf.at[mine], recv_a.at[me]).start()
    pltpu.make_async_copy(w_ref.at[mine], wbuf.at[mine], recv_w.at[me]).start()
    pltpu.make_async_copy(t_ref.at[mine], tbuf.at[mine], recv_t.at[me]).start()

    def launch(waves):
        for m in waves:
            sends[m][1].start()
            sends[m][2].start()

    far = list(range(peers // 2, peers - 2))
    order = [1]
    for m in range(2, peers // 2):
        order += [far.pop(0), m]
    launch(order + far)

    g_in[...] = jnp.zeros_like(g_in)
    g_out[...] = jnp.zeros_like(g_out)
    g_gain[...] = jnp.zeros_like(g_gain)
    g_head[...] = jnp.zeros_like(g_head)
    for load in loads[2:]:
        load.wait()
    gain = gain_ref[...]
    onehot = onehot_f[...].astype(bf16)

    for c in first_edges:
        c.wait_recv()
    sel[0] = dot(onehot, edge_recv[0])
    sel[1] = dot(onehot, edge_recv[1])

    group = 2 * per
    groups = blocks // group

    def forward(i, carry):
        xs, normeds = [], []
        for k in range(group):
            j = i * group + k
            x = lat_ref[rows_smem[0, 0, j]].astype(f32)
            summed = x + 0.5 * shifted(x, sel[0, pl.ds(j, 1), :], sel[1, pl.ds(j, 1), :])
            inv = lax.rsqrt(jnp.mean(summed * summed, axis=-1, keepdims=True) + norm_eps)
            u = summed * inv
            normed = (u * gain).astype(bf16)
            u_s[j] = u
            inv_s[j] = inv
            xs.append(x)
            normeds.append(normed)
        normed = jnp.concatenate(normeds, axis=0)
        normed_s[i] = normed.T
        pre = dot(normed, w_in_ref[...])
        sig = jax.nn.sigmoid(pre)
        act = (pre * sig).astype(bf16)
        act_s[i] = act.T
        slope_s[i] = sig * (1.0 + pre * (1.0 - sig))
        adv = (jnp.concatenate(xs, axis=0) + dot(act, w_out_ref[...])).astype(bf16)
        for k in range(group):
            j, sl = i * group + k, slice(k * cells, (k + 1) * cells)
            pair_s[j, :, 0:channels] = xs[k].astype(bf16)
            pair_s[j, :, channels:] = adv[sl]

        @pl.when(i == groups - 2)
        def _():
            launch([peers - 2])

        return carry

    lax.fori_loop(0, groups, forward, 0)

    eye = lax.broadcasted_iota(jnp.int32, (obs, obs), 0) == lax.broadcasted_iota(
        jnp.int32, (obs, obs), 1
    )
    loss_scale = 1.0 / math.sqrt(obs)

    def backward(i, carry):
        chip, bit = me // 2, 1
        while bit < groups:
            chip = chip + lax.rem(i // bit, 2) * bit * (1 - 2 * ((me // 2 // bit) % 2))
            bit *= 2

        @pl.when(i == groups // 2 - 1)
        def _():
            launch([peers - 1])

        base = chip * group
        span = pl.ds(base, group)
        for s in (2 * chip, 2 * chip + 1):
            part = pl.ds(s * per, per)
            for buf, sem in ((wbuf, recv_w), (tbuf, recv_t), (auxbuf, recv_a)):
                pltpu.make_async_copy(buf.at[part], buf.at[part], sem.at[s]).wait()
        codes, lats = [], []
        for k in range(group):
            code = jnp.where(eye, auxbuf[base + k][0:1, :], 0.0)
            code = jnp.sum(code, axis=1, keepdims=True)
            codes.append(code)
            c = jnp.maximum(code, 0.0)
            both = dot(wbuf[base + k], pair_s[base + k])
            lats.append(((1.0 - c) * both[:, :channels] + c * both[:, channels:]).astype(bf16))
        obs_latent = jnp.concatenate(lats, axis=0)
        code = jnp.concatenate(codes, axis=0)
        c = jnp.maximum(code, 0.0)
        head = head_ref[...]
        predicted = dot(obs_latent, head)
        goals = tbuf[span].reshape(group * obs, head.shape[1]).astype(f32)
        residual = jnp.where(code >= 0.0, predicted - goals, 0.0)
        pred_grad = (residual * loss_scale).astype(bf16)
        g_head[...] += dot(obs_latent, pred_grad, TN)
        obs_grad = dot(pred_grad, head, NT).astype(bf16).astype(f32)
        back = jnp.concatenate([(1.0 - c) * obs_grad, c * obs_grad], axis=1).astype(bf16)
        olds, news = [], []
        for k in range(group):
            both = dot(wbuf[base + k], back[k * obs : (k + 1) * obs], TN).astype(bf16)
            olds.append(both[:, :channels])
            news.append(both[:, channels:])
        tile_new = jnp.concatenate(news, axis=0)
        u = u_s[span].reshape(group * cells, channels)
        g_out[...] += dot(act_s[chip], tile_new)
        pre_grad = (dot(tile_new, w_out_ref[...], NT) * slope_s[chip]).astype(bf16)
        g_in[...] += dot(normed_s[chip], pre_grad)
        normed_grad = dot(pre_grad, w_in_ref[...], NT)
        ng_u = normed_grad * u
        g_gain[...] += jnp.sum(ng_u, axis=0, keepdims=True)
        mean = jnp.mean(ng_u * gain, axis=-1, keepdims=True)
        core = normed_grad * gain - u * mean
        for k in range(group):
            sl = slice(k * cells, (k + 1) * cells)
            sg = inv_s[base + k] * core[sl]
            sg_edge[0, pl.ds(base + k, 1), :] = sg[cells - 1 : cells]
            sg_edge[1, pl.ds(base + k, 1), :] = sg[0:1]
            part_ref[base + k] = (
                olds[k].astype(f32) + news[k].astype(f32) + sg + 0.5 * shifted(sg, 0.0, 0.0)
            )
        return carry

    lax.fori_loop(0, groups, backward, 0)

    edge_send[2] = dot(onehot, sg_edge[0].astype(bf16), TN).astype(bf16)
    edge_send[3] = dot(onehot, sg_edge[1].astype(bf16), TN).astype(bf16)
    last_edges = [edge_copy(1, 0), edge_copy(1, 1)]
    for c in last_edges:
        c.start()


    def pack(acc, grads, tail):
        at = 0
        for grad in grads:
            for first in range(0, grad.shape[1], 128):
                acc[at : at + grad.shape[0], :] = grad[:, first : first + 128].astype(bf16)
                at += grad.shape[0]
        if tail:
            lines = [g_gain[:, i : i + 128] for i in range(0, channels, 128)]
            lines.append(jnp.zeros((16 - len(lines), 128), f32))
            acc[at : at + 16, :] = jnp.concatenate(lines, axis=0).astype(bf16)
            at += 16
        if at < acc.shape[0]:
            acc[at:, :] = jnp.zeros((acc.shape[0] - at, 128), bf16)

    core, rank, ranks = lax.rem(me, 2), me // 2, peers // 2
    sibling = {"lon": me + 1 - 2 * core}
    band_to = [{"band": lax.rem(band + d, bands)} for d in range(1, bands)]
    rank_to = [{"lon": 2 * lax.rem(rank + d, ranks) + core} for d in range(1, ranks)]
    started = []

    def rows_of(start, size):
        return pl.ds(pl.multiple_of(start, 16), size)

    def send(src, dst, sems, chunk, slot, to):
        copy = pltpu.make_async_remote_copy(
            src_ref=src,
            dst_ref=dst,
            send_sem=sems.at[chunk, 0, slot],
            recv_sem=sems.at[chunk, 1, slot],
            device_id=to,
            device_id_type=MESH,
        )
        copy.start()
        started.append(copy)
        return copy

    def arrived(copies):
        for copy in copies:
            copy.wait_recv()

    def reduce_steps(n, chunk):
        acc, from_core, core_sum, from_band, band_sum, from_lon, total = chunk
        half = acc.shape[0] // 2
        quarter = half // bands
        piece = quarter // ranks
        lot = core * half + band * quarter
        got = [send(acc.at[rows_of((1 - core) * half, half)], from_core, core_sems, n, 0, sibling)]
        yield
        arrived(got)
        core_sum[...] = (
            acc[rows_of(core * half, half), :].astype(f32) + from_core[...].astype(f32)
        ).astype(bf16)
        got = []
        for d in range(1, bands):
            src = core_sum.at[rows_of(lax.rem(band + d, bands) * quarter, quarter)]
            got.append(send(src, from_band.at[d - 1], band_sems, n, d - 1, band_to[d - 1]))
        yield
        arrived(got)
        added = core_sum[rows_of(band * quarter, quarter), :].astype(f32)
        for d in range(1, bands):
            added = added + from_band[d - 1].astype(f32)
        band_sum[...] = added.astype(bf16)
        got = []
        for d in range(1, ranks):
            src = band_sum.at[rows_of(lax.rem(rank + d, ranks) * piece, piece)]
            got.append(send(src, from_lon.at[d - 1], lon_sems, n, d - 1, rank_to[d - 1]))
        yield
        arrived(got)
        added = band_sum[rows_of(rank * piece, piece), :].astype(f32)
        for d in range(1, ranks):
            added = added + from_lon[d - 1].astype(f32)
        own = rows_of(lot + rank * piece, piece)
        total[own, :] = added.astype(bf16)
        own = total.at[own]
        got = []
        for d in range(1, ranks):
            got.append(send(own, own, lon_sems, n, ranks + d - 2, rank_to[d - 1]))
        yield
        arrived(got)
        own = total.at[rows_of(lot, quarter)]
        got = []
        for d in range(1, bands):
            got.append(send(own, own, band_sems, n, bands + d - 2, band_to[d - 1]))
        yield
        arrived(got)
        own = total.at[rows_of(core * half, half)]
        got = [send(own, own, core_sems, n, 1, sibling)]
        yield
        arrived(got)
        yield

    pack(chunk_a[0], (g_out,), False)
    steps_a = reduce_steps(0, chunk_a)
    next(steps_a)
    pack(chunk_b[0], (g_in, g_head), True)
    steps_b = reduce_steps(1, chunk_b)
    next(steps_b)

    part_ref[blocks] = jnp.zeros((cells, channels), f32)

    def merge(i, carry):
        j = blocks - 1 - i
        row, later = rows_smem[0, 0, j], blocks
        for other in range(blocks - 1, 0, -1):
            same = (rows_smem[0, 0, other] == row) & (other > j)
            later = jnp.where(same, other, later)
        part_ref[j] = part_ref[j] + part_ref[later]
        return carry

    lax.fori_loop(0, blocks, merge, 0)
    next(steps_a)
    next(steps_b)
    for c in last_edges:
        c.wait_recv()
    edge_f[...] = 0.5 * edge_recv[2:4].astype(f32)

    def gather(r, carry):
        found = blocks
        for j in range(blocks - 1, -1, -1):
            found = jnp.where(rows_smem[0, 0, j] == r, j, found)
        lat_out[r] = part_ref[found]
        lat_out[r, 0:1, :] += edge_f[0, pl.ds(r, 1), :]
        lat_out[r, cells - 1 : cells, :] += edge_f[1, pl.ds(r, 1), :]
        return carry

    lax.fori_loop(0, lat_rows, gather, 0)
    store = pltpu.make_async_copy(lat_out, rows_out, store_sem.at[0])
    store.start()
    for _ in range(5):
        next(steps_a)
        next(steps_b)
    split = chunk_a[0].shape[0]
    stores = [
        pltpu.make_async_copy(chunk_a[-1], sums_ref.at[0:split], store_sem.at[1]),
        pltpu.make_async_copy(chunk_b[-1], sums_ref.at[split:], store_sem.at[2]),
    ]
    for copy in stores:
        copy.start()

    for copy in started + first_edges + last_edges:
        copy.wait_send()
    for m in range(1, peers):
        for copy in sends[m]:
            copy.wait_send()
    for copy in [store] + stores:
        copy.wait()


def layer(latent, rows, weights, slots, counts, targets, gain, w_in, w_out, head, peers, bands):
    lat_rows, cells, channels = latent.shape
    blocks, obs = slots.shape
    hid = w_in.shape[1]
    values = head.shape[1]
    vmem, anym = pl.BlockSpec(memory_space=pltpu.VMEM), pl.BlockSpec(memory_space=pl.ANY)
    smem = pl.BlockSpec(memory_space=pltpu.SMEM)
    shape = jax.ShapeDtypeStruct
    dma = pltpu.SemaphoreType.DMA
    flops = 2 * blocks * cells * channels * (6 * hid + 4 * obs + 3 * values)
    pieces, ranks = bands * peers, peers // 2

    def chunk(lines):
        total = pieces * 16 * pl.cdiv(lines, pieces * 16)
        half, quarter, piece = total // 2, total // 2 // bands, total // pieces
        shapes = [
            (total, 128),
            (half, 128),
            (half, 128),
            (bands - 1, quarter, 128),
            (quarter, 128),
            (ranks - 1, piece, 128),
            (total, 128),
        ]
        return total, tuple(pltpu.VMEM(one, bf16) for one in shapes)

    total_a, chunk_a = chunk(channels * hid // 128)
    total_b, chunk_b = chunk(channels * (hid + values) // 128 + 16)
    return pl.pallas_call(
        functools.partial(layer_kernel, peers, bands),
        out_shape=[
            shape((lat_rows, cells, channels), f32),
            shape((total_a + total_b, 128), bf16),
        ],
        in_specs=[smem] * 2 + [anym] * 8,
        out_specs=[anym, anym],
        scratch_shapes=[
            pltpu.VMEM((blocks + 1, cells, channels), f32),
            pltpu.VMEM((lat_rows, cells, channels), f32),
            pltpu.VMEM(latent.shape, bf16),
            pltpu.VMEM((blocks, obs), jnp.int32),
            pltpu.VMEM((1, channels), f32),
            pltpu.VMEM(w_in.shape, bf16),
            pltpu.VMEM(w_out.shape, bf16),
            pltpu.VMEM(head.shape, bf16),
            pltpu.VMEM(w_in.shape, f32),
            pltpu.VMEM(w_out.shape, f32),
            pltpu.VMEM((1, channels), f32),
            pltpu.VMEM(head.shape, f32),
            pltpu.VMEM((blocks, lat_rows), f32),
            pltpu.VMEM((blocks, obs), f32),
            chunk_a,
            chunk_b,
            pltpu.VMEM((blocks, obs, cells), bf16),
            pltpu.VMEM((blocks, obs, values), bf16),
            pltpu.VMEM((blocks, 8, obs), f32),
            pltpu.VMEM((blocks, 8, obs), f32),
            pltpu.VMEM((2, lat_rows, channels), f32),
            pltpu.VMEM((4, lat_rows, channels), bf16),
            pltpu.VMEM((4, lat_rows, channels), bf16),
            pltpu.VMEM((2, blocks, channels), f32),
            pltpu.VMEM((blocks, cells, channels), f32),
            pltpu.VMEM((blocks, cells, 1), f32),
            pltpu.VMEM((ranks, channels, blocks * cells // ranks), bf16),
            pltpu.VMEM((ranks, hid, blocks * cells // ranks), bf16),
            pltpu.VMEM((ranks, blocks * cells // ranks, hid), f32),
            pltpu.VMEM((blocks, cells, 2 * channels), bf16),
            pltpu.VMEM((2, blocks, channels), f32),
        ]
        + [dma((peers,))] * 6
        + [dma((4,))] * 2
        + [dma((6,)), dma((3,)), dma((2, 2, 2))]
        + [dma((2, 2, 2 * (bands - 1))), dma((2, 2, 2 * (ranks - 1)))],
        compiler_params=pltpu.CompilerParams(
            collective_id=0, has_side_effects=True, vmem_limit_bytes=56 * 1024 * 1024
        ),
        cost_estimate=pl.CostEstimate(
            flops=flops, bytes_accessed=10 * 1024 * 1024, transcendentals=blocks * cells * hid
        ),
    )(
        rows,
        counts,
        latent,
        weights,
        targets,
        slots,
        gain.reshape(1, channels),
        w_in,
        w_out,
        head,
    )


def finish_kernel(
    scale, split, rows_ref, sums_hbm, out_ref, w_in_g, w_out_g, gain_g, head_g, held, sums_ref, sems
):
    count = sems.shape[1] - 1
    size = rows_ref.shape[0] // count
    load = pltpu.make_async_copy(sums_hbm, sums_ref, sems.at[0, count])
    load.start()
    reads, writes = [], []
    for i in range(count):
        part = pl.ds(i * size, size)
        reads.append(pltpu.make_async_copy(rows_ref.at[part], held.at[part], sems.at[0, i]))
        writes.append(pltpu.make_async_copy(held.at[part], out_ref.at[part], sems.at[1, i]))
        reads[-1].start()
    for i in range(count):
        reads[i].wait()
        writes[i].start()
    load.wait()
    at = 0
    for grad in (w_out_g, w_in_g, head_g):
        for lane in range(0, grad.shape[1], 128):
            part = sums_ref[at : at + grad.shape[0], :].astype(f32)
            grad[:, lane : lane + 128] = part * scale
            at += grad.shape[0]
        if grad is w_out_g:
            at = split
    lines = sums_ref[at : at + 16, :].astype(f32) * scale
    for i in range(gain_g.shape[1] // 128):
        gain_g[:, i * 128 : (i + 1) * 128] = lines[i : i + 1]
    for write in writes:
        write.wait()


def finish(rows, sums, w_in, w_out, head, scale, split):
    channels = rows.shape[2]
    vmem, anym = pl.BlockSpec(memory_space=pltpu.VMEM), pl.BlockSpec(memory_space=pl.ANY)
    shape = jax.ShapeDtypeStruct
    return pl.pallas_call(
        functools.partial(finish_kernel, scale, split),
        out_shape=[
            shape(rows.shape, f32),
            shape(w_in.shape, f32),
            shape(w_out.shape, f32),
            shape((1, channels), f32),
            shape(head.shape, f32),
        ],
        in_specs=[anym] * 2,
        out_specs=[anym] + [vmem] * 4,
        scratch_shapes=[
            pltpu.VMEM(rows.shape, f32),
            pltpu.VMEM(sums.shape, bf16),
            pltpu.SemaphoreType.DMA((2, 9)),
        ],
        compiler_params=pltpu.CompilerParams(vmem_limit_bytes=56 * 1024 * 1024),
        cost_estimate=pl.CostEstimate(
            flops=sums.size, bytes_accessed=8 * rows.size + 6 * sums.size, transcendentals=0
        ),
    )(rows, sums)


def body(latent, row_index, weights, slots, counts, targets, gain, w_in, w_out, head):
    peers, bands = lax.axis_size("lon"), lax.axis_size("band")
    split = 16 * bands * peers
    split = split * pl.cdiv(w_in.size // 128, split)
    rows, sums = layer(
        latent, row_index, weights, slots, counts, targets, gain, w_in, w_out, head, peers, bands
    )
    grad_latent, g_in, g_out, g_gain, g_head = finish(
        rows, sums, w_in, w_out, head, 1.0 / (peers * bands), split
    )
    return grad_latent, g_in, g_out, g_gain.reshape(-1), g_head


def solution(mesh):
    return jax.shard_map(
        body,
        mesh=mesh,
        in_specs=(
            P("band", "lon", None),
            P("band", "lon", None),
            P(("band", "lon"), None, None),
            P(("band", "lon"), None),
            P(("band", "lon")),
            P(("band", "lon"), None, None),
            P(),
            P(),
            P(),
            P(),
        ),
        out_specs=(P("band", "lon", None), P(), P(), P(), P()),
        check_vma=False,
    )
```

```python
import functools
import math

import jax
import jax.numpy as jnp
from jax import lax
from jax.experimental import pallas as pl
from jax.experimental.pallas import tpu as pltpu
from jax.sharding import PartitionSpec as P

WINDOW_SLOTS = 7
norm_eps = 1e-05
f32, bf16 = jnp.float32, jnp.bfloat16
MESH = pl.DeviceIdType.MESH


def dot(a, b, dims=((1,), (0,))):
    return lax.dot_general(a, b, (dims, ((), ())), preferred_element_type=f32)


NN = ((1,), (0,))
NT = ((1,), (1,))
TN = ((0,), (0,))


def shifted(x, first, last):
    cells = x.shape[0]
    place = lax.broadcasted_iota(jnp.int32, x.shape, 0)
    before = jnp.where(place == 0, first, pltpu.roll(x, 1, 0))
    after = jnp.where(place == cells - 1, last, pltpu.roll(x, cells - 1, 0))
    return before + after


def layer_kernel(
    peers,
    bands,
    rows_smem,
    count_smem,
    lat_hbm,
    w_ref,
    t_ref,
    slot_hbm,
    gain_hbm,
    w_in_hbm,
    w_out_hbm,
    head_hbm,
    rows_out,
    sums_ref,
    part_ref,
    lat_out,
    lat_ref,
    slot_ref,
    gain_ref,
    w_in_ref,
    w_out_ref,
    head_ref,
    g_in,
    g_out,
    g_gain,
    g_head,
    onehot_f,
    live_f,
    chunk_a,
    chunk_b,
    wbuf,
    tbuf,
    aux,
    auxbuf,
    edge_f,
    edge_send,
    edge_recv,
    sel,
    u_s,
    inv_s,
    normed_s,
    act_s,
    slope_s,
    pair_s,
    sg_edge,
    send_w,
    send_t,
    send_a,
    recv_w,
    recv_t,
    recv_a,
    send_e,
    recv_e,
    load_sem,
    store_sem,
    core_sems,
    band_sems,
    lon_sems,
):
    lat_rows, cells, channels = lat_ref.shape
    blocks, obs = slot_ref.shape
    per = blocks // peers
    me = lax.axis_index("lon")
    band = lax.axis_index("band")
    right, left = lax.rem(me + 1, peers), lax.rem(me + peers - 1, peers)

    def partner(m):
        other, bit = me, 1
        while bit < peers:
            flip = (m // bit) % 2
            other = other + flip * bit * (1 - 2 * ((me // bit) % 2))
            bit *= 2
        return other

    loads = [
        pltpu.make_async_copy(a, b, load_sem.at[i])
        for i, (a, b) in enumerate(
            (
                (slot_hbm, slot_ref),
                (lat_hbm, lat_ref),
                (gain_hbm, gain_ref),
                (w_in_hbm, w_in_ref),
                (w_out_hbm, w_out_ref),
                (head_hbm, head_ref),
            )
        )
    ]
    for load in loads:
        load.start()

    barrier = pltpu.get_barrier_semaphore()
    for d in range(1, peers):
        pl.semaphore_signal(
            barrier, inc=1, device_id={"lon": lax.rem(me + d, peers)}, device_id_type=MESH
        )
    for d in range(1, bands):
        pl.semaphore_signal(
            barrier, inc=1, device_id={"band": lax.rem(band + d, bands)}, device_id_type=MESH
        )
    pl.semaphore_wait(barrier, peers + bands - 2)

    def exchange(m):
        to = partner(m)
        src, dst = pl.ds(to * per, per), pl.ds(me * per, per)
        return [
            pltpu.make_async_remote_copy(
                src_ref=a.at[to if a is aux else src],
                dst_ref=b.at[me if a is aux else dst],
                send_sem=ss.at[to],
                recv_sem=rs.at[me],
                device_id={"lon": to},
                device_id_type=MESH,
            )
            for a, b, ss, rs in (
                (aux, auxbuf, send_a, recv_a),
                (w_ref, wbuf, send_w, recv_w),
                (t_ref, tbuf, send_t, recv_t),
            )
        ]

    sends = [None] + [exchange(m) for m in range(1, peers)]
    mine = pl.ds(me * per, per)

    def launch(waves):
        for m in waves:
            sends[m][1].start()
            sends[m][2].start()

    launch([peers // 2, 1])
    pltpu.make_async_copy(w_ref.at[mine], wbuf.at[mine], recv_w.at[me]).start()
    pltpu.make_async_copy(t_ref.at[mine], tbuf.at[mine], recv_t.at[me]).start()

    lane = lax.broadcasted_iota(jnp.int32, (1, obs), 1)
    row_lane = lax.broadcasted_iota(jnp.int32, (1, lat_rows), 1)
    for j in range(blocks):
        live_f[j : j + 1, :] = (lane < count_smem[j]).astype(f32)
        onehot_f[j : j + 1, :] = (row_lane == rows_smem[0, 0, j]).astype(f32)
    loads[0].wait()
    coef = (slot_ref[...].astype(f32) / (WINDOW_SLOTS - 1)).astype(bf16).astype(f32)
    coded = jnp.where(live_f[...] > 0.0, coef, -1.0)
    aux[...] = jnp.zeros_like(aux)
    for p in range(peers):
        aux[p, 0:per, :] = coded[p * per : (p + 1) * per]
    loads[1].wait()
    for r in range(lat_rows):
        edge_f[0, r : r + 1, :] = lat_ref[r, cells - 16 : cells, :].astype(f32)[15:16]
        edge_f[1, r : r + 1, :] = lat_ref[r, 0:16, :].astype(f32)[0:1]
    edge_send[0:2] = edge_f[...].astype(bf16)

    def edge_copy(phase, side):
        slot = 2 * phase + side
        return pltpu.make_async_remote_copy(
            src_ref=edge_send.at[slot],
            dst_ref=edge_recv.at[slot],
            send_sem=send_e.at[slot],
            recv_sem=recv_e.at[slot],
            device_id={"lon": left if side else right},
            device_id_type=MESH,
        )

    first_edges = [edge_copy(0, 0), edge_copy(0, 1)]
    for c in first_edges:
        c.start()

    for m in range(1, peers):
        sends[m][0].start()
    pltpu.make_async_copy(aux.at[me], auxbuf.at[me], recv_a.at[me]).start()
    order = []
    for m in range(2, peers // 2):
        order += [m + peers // 2 - 1, m]
    launch(order)

    g_in[...] = jnp.zeros_like(g_in)
    g_out[...] = jnp.zeros_like(g_out)
    g_gain[...] = jnp.zeros_like(g_gain)
    g_head[...] = jnp.zeros_like(g_head)
    for load in loads[2:]:
        load.wait()
    gain = gain_ref[...]
    onehot = onehot_f[...].astype(bf16)

    for c in first_edges:
        c.wait_recv()
    sel[0] = dot(onehot, edge_recv[0])
    sel[1] = dot(onehot, edge_recv[1])

    group = 2 * per
    groups = blocks // group

    def forward(i, carry):
        xs, normeds = [], []
        for k in range(group):
            j = i * group + k
            x = lat_ref[rows_smem[0, 0, j]].astype(f32)
            summed = x + 0.5 * shifted(x, sel[0, pl.ds(j, 1), :], sel[1, pl.ds(j, 1), :])
            inv = lax.rsqrt(jnp.mean(summed * summed, axis=-1, keepdims=True) + norm_eps)
            u = summed * inv
            normed = (u * gain).astype(bf16)
            u_s[j] = u
            inv_s[j] = inv
            xs.append(x)
            normeds.append(normed)
        normed = jnp.concatenate(normeds, axis=0)
        normed_s[i] = normed.T
        pre = dot(normed, w_in_ref[...])
        sig = jax.nn.sigmoid(pre)
        act = (pre * sig).astype(bf16)
        act_s[i] = act.T
        slope_s[i] = sig * (1.0 + pre * (1.0 - sig))
        adv = (jnp.concatenate(xs, axis=0) + dot(act, w_out_ref[...])).astype(bf16)
        for k in range(group):
            j, sl = i * group + k, slice(k * cells, (k + 1) * cells)
            pair_s[j, :, 0:channels] = xs[k].astype(bf16)
            pair_s[j, :, channels:] = adv[sl]

        @pl.when(i == groups - 1)
        def _():
            launch([peers - 1])

        return carry

    lax.fori_loop(0, groups, forward, 0)

    eye = lax.broadcasted_iota(jnp.int32, (obs, obs), 0) == lax.broadcasted_iota(
        jnp.int32, (obs, obs), 1
    )
    loss_scale = 1.0 / math.sqrt(obs)

    def backward(i, carry):
        chip, bit = me // 2, 1
        while bit < groups:
            chip = chip + lax.rem(i // bit, 2) * bit * (1 - 2 * ((me // 2 // bit) % 2))
            bit *= 2

        base = chip * group
        span = pl.ds(base, group)
        for s in (2 * chip, 2 * chip + 1):
            part = pl.ds(s * per, per)
            for buf, sem in ((wbuf, recv_w), (tbuf, recv_t)):
                pltpu.make_async_copy(buf.at[part], buf.at[part], sem.at[s]).wait()
            pltpu.make_async_copy(auxbuf.at[s], auxbuf.at[s], recv_a.at[s]).wait()
        codes, lats = [], []
        for k in range(group):
            code = jnp.where(eye, auxbuf[2 * chip + k // per][k % per : k % per + 1, :], 0.0)
            code = jnp.sum(code, axis=1, keepdims=True)
            codes.append(code)
            c = jnp.maximum(code, 0.0)
            both = dot(wbuf[base + k], pair_s[base + k])
            lats.append(((1.0 - c) * both[:, :channels] + c * both[:, channels:]).astype(bf16))
        obs_latent = jnp.concatenate(lats, axis=0)
        code = jnp.concatenate(codes, axis=0)
        c = jnp.maximum(code, 0.0)
        head = head_ref[...]
        predicted = dot(obs_latent, head)
        goals = tbuf[span].reshape(group * obs, head.shape[1]).astype(f32)
        residual = jnp.where(code >= 0.0, predicted - goals, 0.0)
        pred_grad = (residual * loss_scale).astype(bf16)
        g_head[...] += dot(obs_latent, pred_grad, TN)
        obs_grad = dot(pred_grad, head, NT).astype(bf16).astype(f32)
        back = jnp.concatenate([(1.0 - c) * obs_grad, c * obs_grad], axis=1).astype(bf16)
        olds, news = [], []
        for k in range(group):
            both = dot(wbuf[base + k], back[k * obs : (k + 1) * obs], TN).astype(bf16)
            olds.append(both[:, :channels])
            news.append(both[:, channels:])
        tile_new = jnp.concatenate(news, axis=0)
        u = u_s[span].reshape(group * cells, channels)
        g_out[...] += dot(act_s[chip], tile_new)
        pre_grad = (dot(tile_new, w_out_ref[...], NT) * slope_s[chip]).astype(bf16)
        g_in[...] += dot(normed_s[chip], pre_grad)
        normed_grad = dot(pre_grad, w_in_ref[...], NT)
        ng_u = normed_grad * u
        g_gain[...] += jnp.sum(ng_u, axis=0, keepdims=True)
        mean = jnp.mean(ng_u * gain, axis=-1, keepdims=True)
        core = normed_grad * gain - u * mean
        for k in range(group):
            sl = slice(k * cells, (k + 1) * cells)
            sg = inv_s[base + k] * core[sl]
            sg_edge[0, pl.ds(base + k, 1), :] = sg[cells - 1 : cells]
            sg_edge[1, pl.ds(base + k, 1), :] = sg[0:1]
            part_ref[base + k] = (
                olds[k].astype(f32) + news[k].astype(f32) + sg + 0.5 * shifted(sg, 0.0, 0.0)
            )
        return carry

    lax.fori_loop(0, groups, backward, 0)

    edge_send[2] = dot(onehot, sg_edge[0].astype(bf16), TN).astype(bf16)
    edge_send[3] = dot(onehot, sg_edge[1].astype(bf16), TN).astype(bf16)
    last_edges = [edge_copy(1, 0), edge_copy(1, 1)]
    for c in last_edges:
        c.start()


    def pack(acc, grads, tail):
        at = 0
        for grad in grads:
            for first in range(0, grad.shape[1], 128):
                acc[at : at + grad.shape[0], :] = grad[:, first : first + 128].astype(bf16)
                at += grad.shape[0]
        if tail:
            lines = [g_gain[:, i : i + 128] for i in range(0, channels, 128)]
            lines.append(jnp.zeros((16 - len(lines), 128), f32))
            acc[at : at + 16, :] = jnp.concatenate(lines, axis=0).astype(bf16)
            at += 16
        if at < acc.shape[0]:
            acc[at:, :] = jnp.zeros((acc.shape[0] - at, 128), bf16)

    core, rank, ranks = lax.rem(me, 2), me // 2, peers // 2
    sibling = {"lon": me + 1 - 2 * core}
    band_to = [{"band": lax.rem(band + d, bands)} for d in range(1, bands)]
    rank_to = [{"lon": 2 * lax.rem(rank + d, ranks) + core} for d in range(1, ranks)]
    started = []

    def rows_of(start, size):
        return pl.ds(pl.multiple_of(start, 16), size)

    def send(src, dst, sems, chunk, slot, to):
        copy = pltpu.make_async_remote_copy(
            src_ref=src,
            dst_ref=dst,
            send_sem=sems.at[chunk, 0, slot],
            recv_sem=sems.at[chunk, 1, slot],
            device_id=to,
            device_id_type=MESH,
        )
        copy.start()
        started.append(copy)
        return copy

    def arrived(copies):
        for copy in copies:
            copy.wait_recv()

    def reduce_steps(n, chunk):
        acc, from_core, core_sum, from_band, band_sum, from_lon, total = chunk
        half = acc.shape[0] // 2
        quarter = half // bands
        piece = quarter // ranks
        lot = core * half + band * quarter
        got = [send(acc.at[rows_of((1 - core) * half, half)], from_core, core_sems, n, 0, sibling)]
        yield
        arrived(got)
        core_sum[...] = (
            acc[rows_of(core * half, half), :].astype(f32) + from_core[...].astype(f32)
        ).astype(bf16)
        got = []
        for d in range(1, bands):
            src = core_sum.at[rows_of(lax.rem(band + d, bands) * quarter, quarter)]
            got.append(send(src, from_band.at[d - 1], band_sems, n, d - 1, band_to[d - 1]))
        yield
        arrived(got)
        added = core_sum[rows_of(band * quarter, quarter), :].astype(f32)
        for d in range(1, bands):
            added = added + from_band[d - 1].astype(f32)
        band_sum[...] = added.astype(bf16)
        got = []
        for d in range(1, ranks):
            src = band_sum.at[rows_of(lax.rem(rank + d, ranks) * piece, piece)]
            got.append(send(src, from_lon.at[d - 1], lon_sems, n, d - 1, rank_to[d - 1]))
        yield
        arrived(got)
        added = band_sum[rows_of(rank * piece, piece), :].astype(f32)
        for d in range(1, ranks):
            added = added + from_lon[d - 1].astype(f32)
        own = rows_of(lot + rank * piece, piece)
        total[own, :] = added.astype(bf16)
        own = total.at[own]
        got = []
        for d in range(1, ranks):
            got.append(send(own, own, lon_sems, n, ranks + d - 2, rank_to[d - 1]))
        yield
        arrived(got)
        own = total.at[rows_of(lot, quarter)]
        got = []
        for d in range(1, bands):
            got.append(send(own, own, band_sems, n, bands + d - 2, band_to[d - 1]))
        yield
        arrived(got)
        own = total.at[rows_of(core * half, half)]
        got = [send(own, own, core_sems, n, 1, sibling)]
        yield
        arrived(got)
        yield

    pack(chunk_a[0], (g_out,), False)
    steps_a = reduce_steps(0, chunk_a)
    next(steps_a)
    pack(chunk_b[0], (g_in, g_head), True)
    steps_b = reduce_steps(1, chunk_b)
    next(steps_b)

    part_ref[blocks] = jnp.zeros((cells, channels), f32)

    def merge(i, carry):
        j = blocks - 1 - i
        row, later = rows_smem[0, 0, j], blocks
        for other in range(blocks - 1, 0, -1):
            same = (rows_smem[0, 0, other] == row) & (other > j)
            later = jnp.where(same, other, later)
        part_ref[j] = part_ref[j] + part_ref[later]
        return carry

    lax.fori_loop(0, blocks, merge, 0)
    next(steps_a)
    next(steps_b)
    for c in last_edges:
        c.wait_recv()
    edge_f[...] = 0.5 * edge_recv[2:4].astype(f32)

    def gather(r, carry):
        found = blocks
        for j in range(blocks - 1, -1, -1):
            found = jnp.where(rows_smem[0, 0, j] == r, j, found)
        lat_out[r] = part_ref[found]
        lat_out[r, 0:1, :] += edge_f[0, pl.ds(r, 1), :]
        lat_out[r, cells - 1 : cells, :] += edge_f[1, pl.ds(r, 1), :]
        return carry

    lax.fori_loop(0, lat_rows, gather, 0)
    store = pltpu.make_async_copy(lat_out, rows_out, store_sem.at[0])
    store.start()
    for _ in range(5):
        next(steps_a)
        next(steps_b)
    split = chunk_a[0].shape[0]
    stores = [
        pltpu.make_async_copy(chunk_a[-1], sums_ref.at[0:split], store_sem.at[1]),
        pltpu.make_async_copy(chunk_b[-1], sums_ref.at[split:], store_sem.at[2]),
    ]
    for copy in stores:
        copy.start()

    for copy in started + first_edges + last_edges:
        copy.wait_send()
    for m in range(1, peers):
        for copy in sends[m]:
            copy.wait_send()
    for copy in [store] + stores:
        copy.wait()


def layer(latent, rows, weights, slots, counts, targets, gain, w_in, w_out, head, peers, bands):
    lat_rows, cells, channels = latent.shape
    blocks, obs = slots.shape
    per = blocks // peers
    hid = w_in.shape[1]
    values = head.shape[1]
    anym = pl.BlockSpec(memory_space=pl.ANY)
    smem = pl.BlockSpec(memory_space=pltpu.SMEM)
    shape = jax.ShapeDtypeStruct
    dma = pltpu.SemaphoreType.DMA
    flops = 2 * blocks * cells * channels * (6 * hid + 4 * obs + 3 * values)
    pieces, ranks = bands * peers, peers // 2

    def chunk(lines):
        total = pieces * 16 * pl.cdiv(lines, pieces * 16)
        half, quarter, piece = total // 2, total // 2 // bands, total // pieces
        shapes = [
            (total, 128),
            (half, 128),
            (half, 128),
            (bands - 1, quarter, 128),
            (quarter, 128),
            (ranks - 1, piece, 128),
            (total, 128),
        ]
        return total, tuple(pltpu.VMEM(one, bf16) for one in shapes)

    total_a, chunk_a = chunk(channels * hid // 128)
    total_b, chunk_b = chunk(channels * (hid + values) // 128 + 16)
    return pl.pallas_call(
        functools.partial(layer_kernel, peers, bands),
        out_shape=[
            shape((lat_rows, cells, channels), f32),
            shape((total_a + total_b, 128), bf16),
        ],
        in_specs=[smem] * 2 + [anym] * 8,
        out_specs=[anym, anym],
        scratch_shapes=[
            pltpu.VMEM((blocks + 1, cells, channels), f32),
            pltpu.VMEM((lat_rows, cells, channels), f32),
            pltpu.VMEM(latent.shape, bf16),
            pltpu.VMEM((blocks, obs), jnp.int32),
            pltpu.VMEM((1, channels), f32),
            pltpu.VMEM(w_in.shape, bf16),
            pltpu.VMEM(w_out.shape, bf16),
            pltpu.VMEM(head.shape, bf16),
            pltpu.VMEM(w_in.shape, f32),
            pltpu.VMEM(w_out.shape, f32),
            pltpu.VMEM((1, channels), f32),
            pltpu.VMEM(head.shape, f32),
            pltpu.VMEM((blocks, lat_rows), f32),
            pltpu.VMEM((blocks, obs), f32),
            chunk_a,
            chunk_b,
            pltpu.VMEM((blocks, obs, cells), bf16),
            pltpu.VMEM((blocks, obs, values), bf16),
            pltpu.VMEM((peers, 8 * pl.cdiv(per, 8), obs), f32),
            pltpu.VMEM((peers, 8 * pl.cdiv(per, 8), obs), f32),
            pltpu.VMEM((2, lat_rows, channels), f32),
            pltpu.VMEM((4, lat_rows, channels), bf16),
            pltpu.VMEM((4, lat_rows, channels), bf16),
            pltpu.VMEM((2, blocks, channels), f32),
            pltpu.VMEM((blocks, cells, channels), f32),
            pltpu.VMEM((blocks, cells, 1), f32),
            pltpu.VMEM((ranks, channels, blocks * cells // ranks), bf16),
            pltpu.VMEM((ranks, hid, blocks * cells // ranks), bf16),
            pltpu.VMEM((ranks, blocks * cells // ranks, hid), f32),
            pltpu.VMEM((blocks, cells, 2 * channels), bf16),
            pltpu.VMEM((2, blocks, channels), f32),
        ]
        + [dma((peers,))] * 6
        + [dma((4,))] * 2
        + [dma((6,)), dma((3,)), dma((2, 2, 2))]
        + [dma((2, 2, 2 * (bands - 1))), dma((2, 2, 2 * (ranks - 1)))],
        compiler_params=pltpu.CompilerParams(
            collective_id=0, has_side_effects=True, vmem_limit_bytes=56 * 1024 * 1024
        ),
        cost_estimate=pl.CostEstimate(
            flops=flops, bytes_accessed=10 * 1024 * 1024, transcendentals=blocks * cells * hid
        ),
    )(
        rows,
        counts,
        latent,
        weights,
        targets,
        slots,
        gain.reshape(1, channels),
        w_in,
        w_out,
        head,
    )


def finish_kernel(
    scale,
    split,
    rows_ref,
    sums_hbm,
    out_ref,
    w_in_hbm,
    w_out_hbm,
    gain_hbm,
    head_hbm,
    w_in_g,
    w_out_g,
    gain_g,
    head_g,
    held,
    sums_ref,
    sems,
    grad_sems,
):
    count = sems.shape[1] - 1
    size = rows_ref.shape[0] // count
    load = pltpu.make_async_copy(sums_hbm, sums_ref, sems.at[0, count])
    load.start()
    reads, writes = [], []
    for i in range(count):
        part = pl.ds(i * size, size)
        reads.append(pltpu.make_async_copy(rows_ref.at[part], held.at[part], sems.at[0, i]))
        writes.append(pltpu.make_async_copy(held.at[part], out_ref.at[part], sems.at[1, i]))
        reads[-1].start()
    for i in range(count):
        reads[i].wait()
        writes[i].start()
    load.wait()
    at = 0
    for grad in (w_out_g, w_in_g, head_g):
        for lane in range(0, grad.shape[1], 128):
            part = sums_ref[at : at + grad.shape[0], :].astype(f32)
            grad[:, lane : lane + 128] = part * scale
            at += grad.shape[0]
        if grad is w_out_g:
            at = split
    lines = sums_ref[at : at + 16, :].astype(f32) * scale
    for i in range(gain_g.shape[1] // 128):
        gain_g[:, i * 128 : (i + 1) * 128] = lines[i : i + 1]
    pairs = ((w_in_g, w_in_hbm), (w_out_g, w_out_hbm), (gain_g, gain_hbm), (head_g, head_hbm))
    for i, (a, b) in enumerate(pairs):
        writes.append(pltpu.make_async_copy(a, b, grad_sems.at[i]))
        writes[-1].start()
    for write in writes:
        write.wait()


def finish(rows, sums, w_in, w_out, head, scale, split):
    channels = rows.shape[2]
    anym = pl.BlockSpec(memory_space=pl.ANY)
    shape = jax.ShapeDtypeStruct
    return pl.pallas_call(
        functools.partial(finish_kernel, scale, split),
        out_shape=[
            shape(rows.shape, f32),
            shape(w_in.shape, f32),
            shape(w_out.shape, f32),
            shape((1, channels), f32),
            shape(head.shape, f32),
        ],
        in_specs=[anym] * 2,
        out_specs=[anym] * 5,
        scratch_shapes=[
            pltpu.VMEM(w_in.shape, f32),
            pltpu.VMEM(w_out.shape, f32),
            pltpu.VMEM((1, channels), f32),
            pltpu.VMEM(head.shape, f32),
            pltpu.VMEM(rows.shape, f32),
            pltpu.VMEM(sums.shape, bf16),
            pltpu.SemaphoreType.DMA((2, 9)),
            pltpu.SemaphoreType.DMA((4,)),
        ],
        compiler_params=pltpu.CompilerParams(vmem_limit_bytes=56 * 1024 * 1024),
        cost_estimate=pl.CostEstimate(
            flops=sums.size, bytes_accessed=8 * rows.size + 6 * sums.size, transcendentals=0
        ),
    )(rows, sums)


def body(latent, row_index, weights, slots, counts, targets, gain, w_in, w_out, head):
    peers, bands = lax.axis_size("lon"), lax.axis_size("band")
    split = 16 * bands * peers
    split = split * pl.cdiv(w_in.size // 128, split)
    rows, sums = layer(
        latent, row_index, weights, slots, counts, targets, gain, w_in, w_out, head, peers, bands
    )
    grad_latent, g_in, g_out, g_gain, g_head = finish(
        rows, sums, w_in, w_out, head, 1.0 / (peers * bands), split
    )
    return grad_latent, g_in, g_out, g_gain.reshape(-1), g_head


def solution(mesh):
    return jax.shard_map(
        body,
        mesh=mesh,
        in_specs=(
            P("band", "lon", None),
            P("band", "lon", None),
            P(("band", "lon"), None, None),
            P(("band", "lon"), None),
            P(("band", "lon")),
            P(("band", "lon"), None, None),
            P(),
            P(),
            P(),
            P(),
        ),
        out_specs=(P("band", "lon", None), P(), P(), P(), P()),
        check_vma=False,
    )
```
